256 devices in a mesh: ctx: 32 (over x_lo, z, core), tp: 8 (over x_hi, y).
Axes of the slice: x: 4 (x_hi: 2, x_lo: 2; x = x_hi * 2 + x_lo), y: 4, z: 8, core: 2. Of those that a mesh axis runs over, the one named last changes fastest.
Arguments:
- hidden_in: bfloat16 [16384, 5376], P('ctx', 'tp'), may hold values from -30 to 30
- w_query: bfloat16 [5376, 2048], P(None, 'tp'), may hold values from -0.078125 to 0.078125
- w_key: bfloat16 [5376, 1024], P(None, 'tp'), may hold values from -0.078125 to 0.078125
- w_value: bfloat16 [5376, 1024], P(None, 'tp'), may hold values from -0.078125 to 0.078125
- q_gain: float32 [128], replicated, may hold values from 0.5 to 1.5
- k_gain: float32 [128], replicated, may hold values from 0.5 to 1.5
- grad_out: bfloat16 [16384, 2048], P('ctx', 'tp'), may hold values from -24 to 24
Outputs:
- grad_input: bfloat16 [16384, 5376], P('ctx', 'tp')
- grad_wq: float32 [5376, 2048], P('ctx', 'tp')
- grad_wk: float32 [5376, 1024], P('ctx', 'tp')
- grad_wv: float32 [5376, 1024], P('ctx', 'tp')
The draws below stay inside these ranges and needn't reach their ends.
All inputs are finite; a program needn't handle non-finite values.
Results may differ from the reference program's by a relative error of at most 0.034.
Values may be sent and summed in bfloat16 or wider, within the bound.
No kernel may reach another device: no remote copies, remote signals or barrier semaphores. Data moves between devices by JAX's collectives and lax.ppermute only.
A program may use at most 128 MiB of HBM per device.

```python
import math
import jax
import jax.numpy as jnp
from jax import lax

D = 5376
HD = 128
WINDOW = 1024
QH = 16
KH = 8
TOK_DEV = 512
TOKENS = 16384
N_CTX = 32


def draw_hidden_in(key, part):
    key = jax.random.fold_in(key, 11)
    k_base, k_scale = jax.random.split(key, 2)
    levels = jax.random.uniform(k_scale, (TOKENS, 1), jnp.float32, 0.0, 1.0)
    row_scale = 0.5 * jnp.exp(levels * math.log(10.0))
    values = row_scale * jnp.clip(jax.random.normal(k_base, (TOKENS, D), jnp.float32), -6.0, 6.0)
    return values.astype(jnp.bfloat16)


def block_scale(stream_key, extent, shards, smallest, high):
    level, own = 1.0, jax.random.fold_in(stream_key, 6)
    for position, parts in shards:
        heights = jnp.exp(jax.random.uniform(jax.random.fold_in(own, position), (parts,), jnp.float32, smallest / len(shards), high / len(shards)))
        level = level * jnp.repeat(heights, extent[position] // parts).reshape([-1 if axis == position else 1 for axis in range(len(extent))])
    return level


def gaussian(rng, dims, width, bound, cuts=(), held_as=jnp.bfloat16):
    level = block_scale(rng, dims, cuts, -0.22, 0.18) if cuts else 1.0
    values = jax.random.normal(rng, dims, jnp.float32) * width * level
    return jnp.minimum(jnp.maximum(values, -bound), bound).astype(held_as)


def setup_inputs(seed: int = 0) -> dict:
    arg_keys = jax.random.split(jax.random.key(seed), 8)
    hidden_in = draw_hidden_in(jax.random.fold_in(arg_keys[7], 71), 0)
    w_query = gaussian(arg_keys[1], (D, QH * HD), D ** -0.5, 0.078125, ((1, 8),))
    w_key = gaussian(arg_keys[2], (D, KH * HD), D ** -0.5, 0.078125, ((1, 8),))
    w_value = gaussian(arg_keys[3], (D, KH * HD), D ** -0.5, 0.078125, ((1, 8),))
    q_gain = jnp.clip(1.0 + 0.1 * jax.random.normal(arg_keys[4], (HD,), jnp.float32), 0.5, 1.5)
    k_gain = jnp.clip(1.0 + 0.1 * jax.random.normal(arg_keys[5], (HD,), jnp.float32), 0.5, 1.5)
    grad_out = gaussian(arg_keys[6], (TOKENS, QH * HD), 4.0, 24.0, ((0, 32), (1, 8)))
    return {"hidden_in": hidden_in, "w_query": w_query, "w_key": w_key, "w_value": w_value, "q_gain": q_gain, "k_gain": k_gain, "grad_out": grad_out}


query_scale = 1.0 / math.sqrt(168.0)
rope_base = 10000.0
norm_eps = 1e-06

def make_heads(query_in, key_in, value_in, q_gain, k_gain, positions):
    head_dim = query_in.shape[-1]
    half_dim = head_dim // 2
    freqs = jnp.exp(-math.log(rope_base) * (2.0 * jnp.arange(half_dim, dtype=jnp.float32) / head_dim))
    angles = positions.astype(jnp.float32)[:, None] * freqs[None, :]
    cosines = jnp.cos(angles)[:, None, :]
    sines = jnp.sin(angles)[:, None, :]

    def rotate_norm(raw, gain):
        mean_sq = lax.optimization_barrier(jnp.mean(raw * raw, axis=-1, keepdims=True))
        normed = raw * lax.rsqrt(mean_sq + norm_eps) * gain
        front_half = normed[..., :half_dim]
        back_half = normed[..., half_dim:]
        turned = jnp.concatenate([front_half * cosines - back_half * sines, back_half * cosines + front_half * sines], axis=-1)
        return turned.astype(jnp.bfloat16)
    return (rotate_norm(query_in, q_gain), rotate_norm(key_in, k_gain), value_in.astype(jnp.bfloat16))

def attend_block(query_low, keys_f, values_f, first_pos):
    rows = query_low.shape[0]
    head_dim = query_low.shape[2]
    kv_heads = keys_f.shape[1]
    group_size = query_low.shape[1] // kv_heads
    span = keys_f.shape[0]
    query_f = lax.optimization_barrier(query_low).astype(jnp.float32)
    grouped = query_f.reshape(rows, kv_heads, group_size, head_dim)
    scores = jnp.einsum('rkgd,lkd->kgrl', grouped, keys_f) * query_scale
    query_pos = first_pos + lax.iota(jnp.int32, rows)
    key_pos = first_pos - WINDOW + lax.iota(jnp.int32, span)
    offset = query_pos[:, None] - key_pos[None, :]
    inside = (offset >= 0) & (offset < WINDOW) & (key_pos[None, :] >= 0)
    unnorm = jnp.where(inside, jnp.exp(scores), 0.0)
    probs = unnorm / lax.optimization_barrier(jnp.sum(unnorm, axis=-1, keepdims=True))
    probs_low = lax.optimization_barrier(probs.astype(jnp.bfloat16)).astype(jnp.float32)
    output = jnp.einsum('kgrl,lkd->rkgd', probs_low, values_f)
    return output.reshape(rows, kv_heads * group_size * head_dim).astype(jnp.bfloat16)

def attention(query_low, key_low, value_low):
    keys_f = lax.optimization_barrier(key_low).astype(jnp.float32)
    values_f = lax.optimization_barrier(value_low).astype(jnp.float32)
    padding = jnp.zeros((WINDOW,) + keys_f.shape[1:], jnp.float32)
    keys_pad = jnp.concatenate([padding, keys_f], axis=0)
    values_pad = jnp.concatenate([padding, values_f], axis=0)
    blocks = query_low.reshape((N_CTX, TOK_DEV) + query_low.shape[1:])
    indices = jnp.arange(N_CTX, dtype=jnp.int32)

    def one_block(pair):
        index, block = pair
        first_pos = (index * TOK_DEV).astype(jnp.int32)
        keys_blk = lax.dynamic_slice_in_dim(keys_pad, first_pos, WINDOW + TOK_DEV, 0)
        values_blk = lax.dynamic_slice_in_dim(values_pad, first_pos, WINDOW + TOK_DEV, 0)
        return attend_block(block, keys_blk, values_blk, first_pos)
    outputs = lax.map(jax.checkpoint(one_block), (indices, blocks))
    return outputs.reshape(TOKENS, -1)

def reference(hidden_in, w_query, w_key, w_value, q_gain, k_gain, grad_out):
    query_in = jnp.dot(hidden_in, w_query, preferred_element_type=jnp.float32).reshape(TOKENS, QH, HD)
    key_in = jnp.dot(hidden_in, w_key, preferred_element_type=jnp.float32).reshape(TOKENS, KH, HD)
    value_in = jnp.dot(hidden_in, w_value, preferred_element_type=jnp.float32).reshape(TOKENS, KH, HD)
    positions = jnp.arange(TOKENS, dtype=jnp.int32)

    def forward(query_raw, key_raw, value_raw):
        query_low, key_low, value_low = make_heads(query_raw, key_raw, value_raw, q_gain, k_gain, positions)
        return attention(query_low, key_low, value_low)
    attn_out, backward = jax.vjp(forward, query_in, key_in, value_in)
    dq_raw, dk_raw, dv_raw = backward(grad_out)
    grad_q = dq_raw.reshape(TOKENS, QH * HD).astype(jnp.bfloat16)
    grad_k = dk_raw.reshape(TOKENS, KH * HD).astype(jnp.bfloat16)
    grad_v = dv_raw.reshape(TOKENS, KH * HD).astype(jnp.bfloat16)
    contract_cols = (((1,), (1,)), ((), ()))
    input_sum = lax.dot_general(grad_q, w_query, contract_cols, preferred_element_type=jnp.float32)
    input_sum = input_sum + lax.dot_general(grad_k, w_key, contract_cols, preferred_element_type=jnp.float32)
    input_sum = input_sum + lax.dot_general(grad_v, w_value, contract_cols, preferred_element_type=jnp.float32)
    contract_rows = (((0,), (0,)), ((), ()))
    grad_wq = lax.dot_general(hidden_in, grad_q, contract_rows, preferred_element_type=jnp.float32)
    grad_wk = lax.dot_general(hidden_in, grad_k, contract_rows, preferred_element_type=jnp.float32)
    grad_wv = lax.dot_general(hidden_in, grad_v, contract_rows, preferred_element_type=jnp.float32)
    return (input_sum.astype(jnp.bfloat16), grad_wq, grad_wk, grad_wv)
```

```python
import functools
import math

import jax
import jax.numpy as jnp
from jax import lax
from jax.experimental import pallas as pl
from jax.experimental.pallas import tpu as pltpu
from jax.sharding import PartitionSpec as P

WINDOW = 1024
HD = 128
HALF = 64
NY, NXH = 4, 2
NXL, NZ, NC = 2, 8, 2

query_scale = 1.0 / math.sqrt(168.0)
rope_base = 10000.0
norm_eps = 1e-06
f32 = jnp.float32
bf16 = jnp.bfloat16
VMEM = pl.BlockSpec(memory_space=pltpu.VMEM)


def tp_perm(dx, dy):
    return [
        (x * NY + y, ((x + dx) % NXH) * NY + (y + dy) % NY)
        for x in range(NXH)
        for y in range(NY)
    ]


def y_step(v, d):
    return lax.ppermute(v, "tp", tp_perm(0, d))


def x_swap(v):
    return lax.ppermute(v, "tp", tp_perm(1, 0))


def core_swap(v):
    return lax.ppermute(v, "ctx", [(i, i ^ 1) for i in range(NXL * NZ * NC)])


def xlo_swap(v):
    n = NXL * NZ * NC
    return lax.ppermute(v, "ctx", [(i, (i + n // 2) % n) for i in range(n)])


def from_behind(block, distance):
    n = NXL * NZ * NC
    route = [(i - distance, i) for i in range(n) if 0 <= i - distance < n]
    return lax.ppermute(block, "ctx", route)


def gather_tp(own):
    half = own.shape[0] // 2
    below = y_step(own, 1)
    above = y_step(own, -1)
    across = x_swap(own)
    up = y_step(jnp.concatenate([below[:half], across[half:]]), 1)
    down = y_step(jnp.concatenate([across[:half], above[half:]]), -1)
    side = x_swap(jnp.concatenate([below[:half], above[half:]]))
    far = jnp.concatenate([up[:half], down[half:]])
    x_below = jnp.concatenate([side[:half], up[half:]])
    x_above = jnp.concatenate([down[:half], side[half:]])
    far_up = y_step(x_below[:half], 1)
    far_down = y_step(x_above[half:], -1)
    x_far = jnp.concatenate([far_up, far_down])
    return {
        (0, 0): own,
        (0, 3): below,
        (0, 1): above,
        (1, 0): across,
        (0, 2): far,
        (1, 3): x_below,
        (1, 1): x_above,
        (1, 2): x_far,
    }


def unrotate_norm(grad, raw, gain, cos, sin):
    top, bottom = grad[:HALF], grad[HALF:]
    d_normed = jnp.concatenate([top * cos + bottom * sin, bottom * cos - top * sin], axis=0)
    inv = lax.rsqrt(jnp.mean(raw * raw, axis=0, keepdims=True) + norm_eps)
    scaled = d_normed * gain
    along = jnp.mean(raw * scaled, axis=0, keepdims=True)
    return inv * scaled - raw * (inv * inv * inv * along)


def rotate_norm(raw, gain, cos, sin):
    inv = lax.rsqrt(jnp.mean(raw * raw, axis=0, keepdims=True) + norm_eps)
    normed = raw * inv * gain
    top, bottom = normed[:HALF], normed[HALF:]
    return jnp.concatenate([top * cos - bottom * sin, bottom * cos + top * sin], axis=0)


def heads_kernel(raw_ref, qg_ref, kg_ref, cos_ref, sin_ref, q_ref, kv_ref):
    cos, sin = cos_ref[...], sin_ref[...]
    for h in range(2):
        rows = slice(h * HD, (h + 1) * HD)
        q_ref[rows, :] = rotate_norm(raw_ref[rows, :], qg_ref[...], cos, sin).astype(bf16)
    kv_ref[0:HD, :] = rotate_norm(raw_ref[2 * HD : 3 * HD, :], kg_ref[...], cos, sin).astype(bf16)
    kv_ref[HD : 2 * HD, :] = raw_ref[3 * HD : 4 * HD, :].astype(bf16)


def attend_kernel(
    ctx_ref, q_ref, raw_ref, own_ref, m1_ref, m2_ref, go_ref, qg_ref, cos_ref, sin_ref,
    dq_ref, d_own_ref, d_m1_ref, d_m2_ref, e_s, dp_s, dk_s, dv_s,
):
    ctx = ctx_ref[0]
    toks = q_ref.shape[1]
    sub = 256
    cos, sin = cos_ref[...], sin_ref[...]
    blocks = (m2_ref, m1_ref, own_ref)
    for h in range(2):
        rows = slice(h * HD, (h + 1) * HD)
        q_t = q_ref[rows, :]
        q = q_t.T
        go = go_ref[:, rows]
        go_t = go.T
        total = jnp.zeros((1, toks), f32)
        weighted = jnp.zeros((1, toks), f32)
        for b in range(3):
            k = blocks[b][0:HD, :].T
            v = blocks[b][HD : 2 * HD, :].T
            for s0 in range(0, toks, sub):
                at = slice(b * toks + s0, b * toks + s0 + sub)
                s = jnp.dot(k[s0 : s0 + sub], q_t, preferred_element_type=f32) * query_scale
                dp = jnp.dot(v[s0 : s0 + sub], go_t, preferred_element_type=f32).astype(bf16)
                key = lax.broadcasted_iota(jnp.int32, (sub, toks), 0) + s0
                query = lax.broadcasted_iota(jnp.int32, (sub, toks), 1)
                if b == 0:
                    inside = (key > query) & (ctx >= 2)
                elif b == 1:
                    inside = (key >= 0) & (ctx >= 1)
                else:
                    inside = key <= query
                e = jnp.where(inside, jnp.exp(s), 0.0)
                e_s[at, :] = e
                dp_s[at, :] = dp
                total = total + jnp.sum(e, axis=0, keepdims=True)
                weighted = weighted + jnp.sum(e * dp.astype(f32), axis=0, keepdims=True)
        inv = 1.0 / total
        weighted = weighted * inv
        dq_t = jnp.zeros((HD, toks), f32)
        for b in range(3):
            for s0 in range(0, toks, sub):
                at = slice(b * toks + s0, b * toks + s0 + sub)
                p = e_s[at, :] * inv
                ds = (p * (dp_s[at, :].astype(f32) - weighted) * query_scale).astype(bf16)
                dv = jnp.dot(p.astype(bf16), go, preferred_element_type=f32)
                dk = jnp.dot(ds, q, preferred_element_type=f32)
                dq_t = dq_t + jnp.dot(
                    blocks[b][0:HD, s0 : s0 + sub], ds, preferred_element_type=f32
                )
                if h == 0:
                    dk_s[at, :] = dk
                    dv_s[at, :] = dv
                else:
                    out = (d_m2_ref, d_m1_ref, d_own_ref)[b]
                    out[0, s0 : s0 + sub, :] = (dk_s[at, :] + dk).astype(out.dtype)
                    out[1, s0 : s0 + sub, :] = (dv_s[at, :] + dv).astype(out.dtype)
        dq_low = dq_t.astype(bf16).astype(f32)
        dq_ref[rows, :] = unrotate_norm(dq_low, raw_ref[rows, :], qg_ref[...], cos, sin).astype(bf16)


def finish_kernel(own_ref, r1_ref, r2_ref, raw_ref, kg_ref, cos_ref, sin_ref, out_ref):
    def total(i):
        t = own_ref[i] + r1_ref[i].astype(f32) + r2_ref[i].astype(f32)
        return t.T.astype(bf16).astype(f32)

    out_ref[0:HD, :] = unrotate_norm(
        total(0), raw_ref[...], kg_ref[...], cos_ref[...], sin_ref[...]
    ).astype(bf16)
    out_ref[HD : 2 * HD, :] = total(1).astype(bf16)


def call(kernel, outs, scratch=(), smem_first=False):
    def run(*args):
        in_specs = [VMEM] * len(args)
        if smem_first:
            in_specs[0] = pl.BlockSpec(memory_space=pltpu.SMEM)
        return pl.pallas_call(
            kernel,
            out_shape=outs,
            in_specs=in_specs,
            out_specs=jax.tree.map(lambda _: VMEM, outs),
            scratch_shapes=list(scratch),
            compiler_params=pltpu.CompilerParams(vmem_limit_bytes=40 * 2**20),
        )(*args)

    return run


def shards(hidden_in, w_query, w_key, w_value, q_gain, k_gain, grad_out):
    toks, feats = hidden_in.shape
    sds = jax.ShapeDtypeStruct
    ctx = lax.axis_index("ctx")
    tp = lax.axis_index("tp")
    core = ctx % NC
    xh, y = tp // NY, tp % NY
    n_tp = NXH * NY
    n_j = NXL * NZ
    blk = feats // 4

    def owner(rel):
        return ((xh + rel[0]) % NXH) * NY + (y + rel[1]) % NY

    positions = ctx * toks + lax.iota(jnp.int32, toks)
    freqs = jnp.exp(-math.log(rope_base) * (2.0 * jnp.arange(HALF, dtype=f32) / HD))
    angles = freqs[:, None] * positions.astype(f32)[None, :]
    cos, sin = jnp.cos(angles), jnp.sin(angles)
    qg, kg = q_gain[:, None], k_gain[:, None]

    w_cat = jnp.concatenate([w_query, w_key, w_value], axis=1)
    cols = w_cat.shape[1]
    w_own = w_cat.reshape(n_tp, feats, cols)

    j = ctx // NC
    part = lax.dynamic_slice(w_own, (0, (j // 4) * blk, (j % 4) * HD), (n_tp, blk, HD))
    part = lax.all_to_all(part, "tp", 0, 0, tiled=True)
    same_core = [[i * NC + c for i in range(n_j)] for c in range(NC)]
    w_rows = lax.all_gather(part, "ctx", axis=0, tiled=False, axis_index_groups=same_core)
    w_rows = w_rows.reshape(4, 4, n_tp, blk, HD).transpose(2, 0, 3, 1, 4).reshape(n_tp, feats, cols)

    x_parts = gather_tp(hidden_in.T)
    raw = None
    x_all = jnp.zeros((n_tp, feats, toks), bf16)
    for rel, xs in x_parts.items():
        at = owner(rel)
        ws = lax.dynamic_index_in_dim(w_own, at, 0, keepdims=False)
        term = lax.dot_general(ws, xs, (((0,), (0,)), ((), ())), preferred_element_type=f32)
        raw = term if raw is None else raw + term
        x_all = lax.dynamic_update_slice(x_all, xs[None], (at, 0, 0))

    q_t, kv_t = call(heads_kernel, (sds((2 * HD, toks), bf16), sds((2 * HD, toks), bf16)))(
        raw, qg, kg, cos, sin
    )
    kv1 = from_behind(kv_t, 1)
    kv2 = from_behind(kv_t, 2)
    pair = sds((2, toks, HD), bf16)
    dq_raw, d_own, d1, d2 = call(
        attend_kernel,
        (sds((2 * HD, toks), bf16), sds((2, toks, HD), f32), pair, pair),
        (
            pltpu.VMEM((3 * toks, toks), f32),
            pltpu.VMEM((3 * toks, toks), bf16),
            pltpu.VMEM((3 * toks, HD), f32),
            pltpu.VMEM((3 * toks, HD), f32),
        ),
        smem_first=True,
    )(ctx[None], q_t, raw[: 2 * HD], kv_t, kv1, kv2, grad_out, qg, cos, sin)
    r1 = from_behind(d1, -1)
    r2 = from_behind(d2, -2)
    dkv_raw = call(finish_kernel, sds((2 * HD, toks), bf16))(
        d_own, r1, r2, raw[2 * HD : 3 * HD], kg, cos, sin
    )

    x_all = x_all.reshape(n_j, NC, blk, toks)
    mine = lax.dynamic_index_in_dim(x_all, core, 1, keepdims=False)
    other = core_swap(lax.dynamic_index_in_dim(x_all, 1 - core, 1, keepdims=False))
    rings = [[(a * NZ + z) * NC + c for z in range(NZ)] for a in range(NXL) for c in range(NC)]
    xl = j // NZ

    def weight_grad(d_t):
        d_other = core_swap(d_t)
        contract = (((2,), (1,)), ((), ()))
        g = lax.dot_general(mine, d_t, contract, preferred_element_type=f32)
        g = g + lax.dot_general(other, d_other, contract, preferred_element_type=f32)
        g = g.astype(bf16).reshape(NXL, NZ, blk, -1).transpose(1, 0, 2, 3)
        g = lax.psum_scatter(
            g, "ctx", scatter_dimension=0, tiled=True, axis_index_groups=rings
        )[0]
        keep = lax.dynamic_index_in_dim(g, xl, 0, keepdims=False)
        send = lax.dynamic_index_in_dim(g, 1 - xl, 0, keepdims=False)
        return keep.astype(f32) + xlo_swap(send).astype(f32)

    grad_wq = weight_grad(dq_raw)
    grad_wkv = weight_grad(dkv_raw)

    total = None
    for d_t, first in ((dq_raw, 0), (dkv_raw, 2 * HD)):
        for rel, ds in gather_tp(d_t).items():
            ws = lax.dynamic_index_in_dim(w_rows, owner(rel), 0, keepdims=False)
            term = jnp.dot(ws[:, first : first + 2 * HD], ds, preferred_element_type=f32)
            total = term if total is None else total + term
    grad_input = total.astype(bf16).T
    return (grad_input, grad_wq, grad_wkv[:, :HD], grad_wkv[:, HD:])


def solution(mesh):
    placed = (P("ctx", "tp"), P(None, "tp"), P(None, "tp"), P(None, "tp"), P(), P(), P("ctx", "tp"))
    return jax.shard_map(
        shards,
        mesh=mesh,
        in_specs=placed,
        out_specs=(P("ctx", "tp"), P("ctx", "tp"), P("ctx", "tp"), P("ctx", "tp")),
        check_vma=False,
    )
```

```python
import functools
import math

import jax
import jax.numpy as jnp
from jax import lax
from jax.experimental import pallas as pl
from jax.experimental.pallas import tpu as pltpu
from jax.sharding import PartitionSpec as P

WINDOW = 1024
HD = 128
HALF = 64
NY, NXH = 4, 2
NXL, NZ, NC = 2, 8, 2

query_scale = 1.0 / math.sqrt(168.0)
rope_base = 10000.0
norm_eps = 1e-06
f32 = jnp.float32
bf16 = jnp.bfloat16
VMEM = pl.BlockSpec(memory_space=pltpu.VMEM)


def tp_perm(dx, dy):
    return [
        (x * NY + y, ((x + dx) % NXH) * NY + (y + dy) % NY)
        for x in range(NXH)
        for y in range(NY)
    ]


def y_step(v, d):
    return lax.ppermute(v, "tp", tp_perm(0, d))


def x_swap(v):
    return lax.ppermute(v, "tp", tp_perm(1, 0))


def core_swap(v):
    return lax.ppermute(v, "ctx", [(i, i ^ 1) for i in range(NXL * NZ * NC)])


def xlo_swap(v):
    n = NXL * NZ * NC
    return lax.ppermute(v, "ctx", [(i, (i + n // 2) % n) for i in range(n)])


def from_behind(block, distance):
    n = NXL * NZ * NC
    route = [(i - distance, i) for i in range(n) if 0 <= i - distance < n]
    return lax.ppermute(block, "ctx", route)


def z_step(v, d):
    route = [
        ((a * NZ + z) * NC + c, (a * NZ + (z + d) % NZ) * NC + c)
        for a in range(NXL)
        for z in range(NZ)
        for c in range(NC)
    ]
    return lax.ppermute(v, "ctx", route)


def tie(values, *after):
    return lax.optimization_barrier((*values, *after))[: len(values)]


RELS = [(0, 0), (0, 3), (0, 1), (1, 0), (0, 2), (1, 3), (1, 1), (1, 2)]


def gather_tp(own, beside_second):
    half = own.shape[0] // 2
    below = y_step(own, 1)
    above = y_step(own, -1)
    across = x_swap(own)
    second = (
        jnp.concatenate([below[:half], across[half:]]),
        jnp.concatenate([across[:half], above[half:]]),
        jnp.concatenate([below[:half], above[half:]]),
    )
    up = y_step(second[0], 1)
    down = y_step(second[1], -1)
    side = x_swap(second[2])
    far = jnp.concatenate([up[:half], down[half:]])
    x_below = jnp.concatenate([side[:half], up[half:]])
    x_above = jnp.concatenate([down[:half], side[half:]])
    third = tie((side[:half], side[half:]), beside_second([own, below, above, across]))
    far_up = y_step(third[0], 1)
    far_down = y_step(third[1], -1)
    x_far = jnp.concatenate([far_up, far_down])
    return [own, below, above, across, far, x_below, x_above, x_far]


def scatter_tp(terms):
    far_x = terms([(1, 2)])[0].astype(bf16)
    half = far_x.shape[0] // 2
    near = terms([(1, 3), (1, 1), (0, 2)])
    top = y_step(far_x[:half], -1)
    bottom = y_step(far_x[half:], 1)
    top, bottom, *near = lax.optimization_barrier((top, bottom, *near))
    x_below, x_above, far = near
    low = lambda *v: jnp.concatenate([u.astype(bf16) for u in v])
    side = x_swap(low(x_below[:half] + top.astype(f32), x_above[half:] + bottom.astype(f32)))
    down = y_step(low(far[:half], x_below[half:]), -1)
    up = y_step(low(x_above[:half], far[half:]), 1)
    last = terms([(0, 3), (0, 1), (1, 0), (0, 0)])
    side, down, up, *last = lax.optimization_barrier((side, down, up, *last))
    below, above, across, own = last
    side, down, up = side.astype(f32), down.astype(f32), up.astype(f32)
    got = (
        y_step(low(below[:half] + side[:half] + down[:half], below[half:]), -1),
        y_step(low(above[:half], above[half:] + side[half:] + up[half:]), 1),
        x_swap(low(across[:half] + up[:half], across[half:] + down[half:])),
    )
    return own + got[0].astype(f32) + got[1].astype(f32) + got[2].astype(f32)


def unrotate_norm(grad, raw, gain, cos, sin):
    top, bottom = grad[:HALF], grad[HALF:]
    d_normed = jnp.concatenate([top * cos + bottom * sin, bottom * cos - top * sin], axis=0)
    inv = lax.rsqrt(jnp.mean(raw * raw, axis=0, keepdims=True) + norm_eps)
    scaled = d_normed * gain
    along = jnp.mean(raw * scaled, axis=0, keepdims=True)
    return inv * scaled - raw * (inv * inv * inv * along)


def rotate_norm(raw, gain, cos, sin):
    inv = lax.rsqrt(jnp.mean(raw * raw, axis=0, keepdims=True) + norm_eps)
    normed = raw * inv * gain
    top, bottom = normed[:HALF], normed[HALF:]
    return jnp.concatenate([top * cos - bottom * sin, bottom * cos + top * sin], axis=0)


def heads_kernel(raw_ref, qg_ref, kg_ref, cos_ref, sin_ref, q_ref, kv_ref):
    cos, sin = cos_ref[...], sin_ref[...]
    for h in range(2):
        rows = slice(h * HD, (h + 1) * HD)
        q_ref[rows, :] = rotate_norm(raw_ref[rows, :], qg_ref[...], cos, sin).astype(bf16)
    kv_ref[0:HD, :] = rotate_norm(raw_ref[2 * HD : 3 * HD, :], kg_ref[...], cos, sin).astype(bf16)
    kv_ref[HD : 2 * HD, :] = raw_ref[3 * HD : 4 * HD, :].astype(bf16)


def attend_kernel(
    ctx_ref, q_ref, raw_ref, own_ref, m1_ref, m2_ref, go_ref, qg_ref, cos_ref, sin_ref,
    dq_ref, d_own_ref, d_m1_ref, d_m2_ref, e_s, dp_s, dk_s, dv_s,
):
    ctx = ctx_ref[0]
    toks = q_ref.shape[1]
    sub = 256
    cos, sin = cos_ref[...], sin_ref[...]
    blocks = (m2_ref, m1_ref, own_ref)
    for h in range(2):
        rows = slice(h * HD, (h + 1) * HD)
        q_t = q_ref[rows, :]
        q = q_t.T
        go = go_ref[:, rows]
        go_t = go.T
        total = jnp.zeros((1, toks), f32)
        weighted = jnp.zeros((1, toks), f32)
        for b in range(3):
            k = blocks[b][0:HD, :].T
            v = blocks[b][HD : 2 * HD, :].T
            for s0 in range(0, toks, sub):
                at = slice(b * toks + s0, b * toks + s0 + sub)
                s = jnp.dot(k[s0 : s0 + sub], q_t, preferred_element_type=f32) * query_scale
                dp = jnp.dot(v[s0 : s0 + sub], go_t, preferred_element_type=f32).astype(bf16)
                key = lax.broadcasted_iota(jnp.int32, (sub, toks), 0) + s0
                query = lax.broadcasted_iota(jnp.int32, (sub, toks), 1)
                if b == 0:
                    inside = (key > query) & (ctx >= 2)
                elif b == 1:
                    inside = (key >= 0) & (ctx >= 1)
                else:
                    inside = key <= query
                e = jnp.where(inside, jnp.exp(s), 0.0)
                e_s[at, :] = e
                dp_s[at, :] = dp
                total = total + jnp.sum(e, axis=0, keepdims=True)
                weighted = weighted + jnp.sum(e * dp.astype(f32), axis=0, keepdims=True)
        inv = 1.0 / total
        weighted = weighted * inv
        dq_t = jnp.zeros((HD, toks), f32)
        for b in range(3):
            for s0 in range(0, toks, sub):
                at = slice(b * toks + s0, b * toks + s0 + sub)
                p = e_s[at, :] * inv
                ds = (p * (dp_s[at, :].astype(f32) - weighted) * query_scale).astype(bf16)
                dv = jnp.dot(p.astype(bf16), go, preferred_element_type=f32)
                dk = jnp.dot(ds, q, preferred_element_type=f32)
                dq_t = dq_t + jnp.dot(
                    blocks[b][0:HD, s0 : s0 + sub], ds, preferred_element_type=f32
                )
                if h == 0:
                    dk_s[at, :] = dk
                    dv_s[at, :] = dv
                else:
                    out = (d_m2_ref, d_m1_ref, d_own_ref)[b]
                    out[0, s0 : s0 + sub, :] = (dk_s[at, :] + dk).astype(out.dtype)
                    out[1, s0 : s0 + sub, :] = (dv_s[at, :] + dv).astype(out.dtype)
        dq_low = dq_t.astype(bf16).astype(f32)
        dq_ref[rows, :] = unrotate_norm(dq_low, raw_ref[rows, :], qg_ref[...], cos, sin).astype(bf16)


def finish_kernel(own_ref, r1_ref, r2_ref, raw_ref, kg_ref, cos_ref, sin_ref, out_ref):
    def total(i):
        t = own_ref[i] + r1_ref[i].astype(f32) + r2_ref[i].astype(f32)
        return t.T.astype(bf16).astype(f32)

    out_ref[0:HD, :] = unrotate_norm(
        total(0), raw_ref[...], kg_ref[...], cos_ref[...], sin_ref[...]
    ).astype(bf16)
    out_ref[HD : 2 * HD, :] = total(1).astype(bf16)


def call(kernel, outs, scratch=(), smem_first=False):
    def run(*args):
        in_specs = [VMEM] * len(args)
        if smem_first:
            in_specs[0] = pl.BlockSpec(memory_space=pltpu.SMEM)
        return pl.pallas_call(
            kernel,
            out_shape=outs,
            in_specs=in_specs,
            out_specs=jax.tree.map(lambda _: VMEM, outs),
            scratch_shapes=list(scratch),
            compiler_params=pltpu.CompilerParams(vmem_limit_bytes=40 * 2**20),
        )(*args)

    return run


def shards(hidden_in, w_query, w_key, w_value, q_gain, k_gain, grad_out):
    toks, feats = hidden_in.shape
    sds = jax.ShapeDtypeStruct
    ctx = lax.axis_index("ctx")
    tp = lax.axis_index("tp")
    core, j = ctx % NC, ctx // NC
    xh, y = tp // NY, tp % NY
    n_tp = NXH * NY
    blk = feats // 4

    def owner(rel):
        return ((xh + rel[0]) % NXH) * NY + (y + rel[1]) % NY

    positions = ctx * toks + lax.iota(jnp.int32, toks)
    freqs = jnp.exp(-math.log(rope_base) * (2.0 * jnp.arange(HALF, dtype=f32) / HD))
    angles = freqs[:, None] * positions.astype(f32)[None, :]
    cos, sin = jnp.cos(angles), jnp.sin(angles)
    qg, kg = q_gain[:, None], k_gain[:, None]

    w_cat = jnp.concatenate([w_query, w_key, w_value], axis=1)
    w_own = w_cat.reshape(n_tp, feats, w_cat.shape[1])

    def project(total, parts, rels):
        for xs, rel in zip(parts, rels):
            ws = lax.dynamic_index_in_dim(w_own, owner(rel), 0, keepdims=False)
            term = lax.dot_general(ws, xs, (((0,), (0,)), ((), ())), preferred_element_type=f32)
            total = term if total is None else total + term
        return total

    begun = []

    def beside(parts):
        begun.append(project(None, parts, RELS[:4]))
        return begun[0]

    x_parts = gather_tp(hidden_in.T, beside)
    most = project(begun[0], x_parts[4:7], RELS[4:7])
    last, most = lax.optimization_barrier((x_parts[7], most))
    raw = project(most, [last], RELS[7:])

    q_t, kv_t = call(heads_kernel, (sds((2 * HD, toks), bf16), sds((2 * HD, toks), bf16)))(
        raw, qg, kg, cos, sin
    )
    kv1 = from_behind(kv_t, 1)
    kv2 = from_behind(kv_t, 2)
    pair = sds((2, toks, HD), bf16)
    dq_raw, d_own, d1, d2 = call(
        attend_kernel,
        (sds((2 * HD, toks), bf16), sds((2, toks, HD), f32), pair, pair),
        (
            pltpu.VMEM((3 * toks, toks), f32),
            pltpu.VMEM((3 * toks, toks), bf16),
            pltpu.VMEM((3 * toks, HD), f32),
            pltpu.VMEM((3 * toks, HD), f32),
        ),
        smem_first=True,
    )(ctx[None], q_t, raw[: 2 * HD], kv_t, kv1, kv2, grad_out, qg, cos, sin)
    r1 = from_behind(d1, -1)
    r2 = from_behind(d2, -2)
    dkv_raw = call(finish_kernel, sds((2 * HD, toks), bf16))(
        d_own, r1, r2, raw[2 * HD : 3 * HD], kg, cos, sin
    )

    x_parts = tie(x_parts, kv_t)
    x_all = jnp.zeros((NY, 2, NC, NXH, blk, toks), bf16)
    for xs, rel in zip(x_parts, RELS):
        t = owner(rel)
        x_all = lax.dynamic_update_slice(
            x_all, xs.reshape(1, 2, NC, 1, blk, toks), (t % NY, 0, 0, t // NY, 0, 0)
        )
    mine = lax.dynamic_index_in_dim(x_all, core, 2, keepdims=False)
    other = core_swap(lax.dynamic_index_in_dim(x_all, 1 - core, 2, keepdims=False))
    mine = mine.reshape(NZ, NXL * blk, toks)
    other = other.reshape(NZ, NXL * blk, toks)
    rings = [[(a * NZ + z) * NC + c for z in range(NZ)] for a in range(NXL) for c in range(NC)]
    xl, z = j // NZ, j % NZ

    def weight_grad(d_t):
        d_other = core_swap(d_t)
        contract = (((2,), (1,)), ((), ()))
        g = lax.dot_general(mine, d_t, contract, preferred_element_type=f32)
        return g + lax.dot_general(other, d_other, contract, preferred_element_type=f32)

    def across_x(g):
        g = g.reshape(NXL, blk, -1)
        keep = lax.dynamic_index_in_dim(g, xl, 0, keepdims=False)
        send = lax.dynamic_index_in_dim(g, 1 - xl, 0, keepdims=False)
        return keep.astype(f32) + xlo_swap(send.astype(bf16)).astype(f32)

    def ring(g):
        own = lambda d: lax.dynamic_index_in_dim(g, (z + d) % NZ, 0, keepdims=False)
        right, left = own(4).astype(bf16), own(5).astype(bf16)
        for step in range(1, 4):
            right = z_step(right, 1)
            right = (own(4 - step) + right.astype(f32)).astype(bf16)
            left = z_step(left, -1)
            if step < 3:
                left = (own(NZ - 3 + step) + left.astype(f32)).astype(bf16)
        right = z_step(right, 1)
        return own(0) + right.astype(f32) + left.astype(f32)

    g_q = weight_grad(dq_raw).astype(bf16)
    g_q = lax.psum_scatter(g_q, "ctx", scatter_dimension=0, tiled=True, axis_index_groups=rings)
    grad_wq = across_x(g_q[0])
    grad_wkv = across_x(ring(weight_grad(dkv_raw)))

    d_all = jnp.concatenate([dq_raw, dkv_raw])

    def terms(rels):
        pick = lambda rel: lax.dynamic_index_in_dim(w_own, owner(rel), 0, keepdims=False)
        return [jnp.dot(pick(rel), d_all, preferred_element_type=f32) for rel in rels]

    grad_input = scatter_tp(terms).astype(bf16).T
    return (grad_input, grad_wq, grad_wkv[:, :HD], grad_wkv[:, HD:])


def solution(mesh):
    placed = (P("ctx", "tp"), P(None, "tp"), P(None, "tp"), P(None, "tp"), P(), P(), P("ctx", "tp"))
    return jax.shard_map(
        shards,
        mesh=mesh,
        in_specs=placed,
        out_specs=(P("ctx", "tp"), P("ctx", "tp"), P("ctx", "tp"), P("ctx", "tp")),
        check_vma=False,
    )
```

```python
import functools
import math

import jax
import jax.numpy as jnp
from jax import lax
from jax.experimental import pallas as pl
from jax.experimental.pallas import tpu as pltpu
from jax.sharding import PartitionSpec as P

WINDOW = 1024
HD = 128
HALF = 64
NY, NXH = 4, 2
NXL, NZ, NC = 2, 8, 2

query_scale = 1.0 / math.sqrt(168.0)
rope_base = 10000.0
norm_eps = 1e-06
f32 = jnp.float32
bf16 = jnp.bfloat16
VMEM = pl.BlockSpec(memory_space=pltpu.VMEM)


def tp_perm(dx, dy):
    return [
        (x * NY + y, ((x + dx) % NXH) * NY + (y + dy) % NY)
        for x in range(NXH)
        for y in range(NY)
    ]


def y_step(v, d):
    return lax.ppermute(v, "tp", tp_perm(0, d))


def x_swap(v):
    return lax.ppermute(v, "tp", tp_perm(1, 0))


def core_swap(v):
    return lax.ppermute(v, "ctx", [(i, i ^ 1) for i in range(NXL * NZ * NC)])


def xlo_swap(v):
    n = NXL * NZ * NC
    return lax.ppermute(v, "ctx", [(i, (i + n // 2) % n) for i in range(n)])


def from_behind(block, distance):
    n = NXL * NZ * NC
    route = [(i - distance, i) for i in range(n) if 0 <= i - distance < n]
    return lax.ppermute(block, "ctx", route)


def tie(values, *after):
    return lax.optimization_barrier((*values, *after))[: len(values)]


RELS = [(0, 0), (0, 3), (0, 1), (1, 0), (0, 2), (1, 3), (1, 1), (1, 2)]
SENT = [(1, 2), (0, 2), (1, 3), (1, 1), (1, 0), (0, 3), (0, 1), (0, 0)]


def gather_tp(own, beside_second):
    half = own.shape[0] // 2
    below = y_step(own, 1)
    above = y_step(own, -1)
    across = x_swap(own)
    second = (
        jnp.concatenate([below[:half], across[half:]]),
        jnp.concatenate([across[:half], above[half:]]),
        jnp.concatenate([below[:half], above[half:]]),
    )
    up = y_step(second[0], 1)
    down = y_step(second[1], -1)
    side = x_swap(second[2])
    far = jnp.concatenate([up[:half], down[half:]])
    x_below = jnp.concatenate([side[:half], up[half:]])
    x_above = jnp.concatenate([down[:half], side[half:]])
    third = tie((side[:half], side[half:]), *beside_second([own, below, above, across]))
    far_up = y_step(third[0], 1)
    far_down = y_step(third[1], -1)
    x_far = jnp.concatenate([far_up, far_down])
    return [own, below, above, across, far, x_below, x_above, x_far]


def cost(us):
    return pl.CostEstimate(flops=0, bytes_accessed=int(us * 3.4e6), transcendentals=0)


def call(kernel, outs, us, scratch=(), smem_first=False, mib=40):
    def run(*args):
        in_specs = [VMEM] * len(args)
        if smem_first:
            in_specs[0] = pl.BlockSpec(memory_space=pltpu.SMEM)
        return pl.pallas_call(
            kernel,
            out_shape=outs,
            in_specs=in_specs,
            out_specs=jax.tree.map(lambda _: VMEM, outs),
            scratch_shapes=list(scratch),
            compiler_params=pltpu.CompilerParams(vmem_limit_bytes=mib * 2**20),
            cost_estimate=cost(us),
        )(*args)

    return run


def halves(ref):
    half = ref.shape[-2] // 2
    return slice(0, half), slice(half, 2 * half)


def add_pair(keep_ref, got_ref, q_ref, k_ref, v_ref):
    total = keep_ref[...].astype(f32) + got_ref[...].astype(f32)
    q_ref[...] = total[:, : 2 * HD]
    k_ref[...] = total[:, 2 * HD : 3 * HD]
    v_ref[...] = total[:, 3 * HD :]


def head_terms(w_ref, dq_ref, dkv_ref):
    width = dq_ref.shape[0]
    t = jnp.dot(w_ref[0, :, :width], dq_ref[...], preferred_element_type=f32)
    return t + jnp.dot(w_ref[0, :, width:], dkv_ref[...], preferred_element_type=f32)


def first_terms(own_ref, w_ref, dq_ref, dkv_ref, top_ref, bottom_ref):
    t = head_terms(w_ref, dq_ref, dkv_ref).astype(bf16)
    lo, hi = halves(w_ref)
    top_ref[...] = t[lo]
    bottom_ref[...] = t[hi]


def second_terms(own_ref, w_ref, dq_ref, dkv_ref, side_ref, down_ref, up_ref):
    lo, hi = halves(w_ref)
    i = pl.program_id(0)
    t = head_terms(w_ref, dq_ref, dkv_ref).astype(bf16)

    @pl.when(i == 0)
    def _():
        down_ref[lo, :] = t[lo]
        up_ref[hi, :] = t[hi]

    @pl.when(i == 1)
    def _():
        side_ref[lo, :] = t[lo]
        down_ref[hi, :] = t[hi]

    @pl.when(i == 2)
    def _():
        up_ref[lo, :] = t[lo]
        side_ref[hi, :] = t[hi]


def third_terms(own_ref, w_ref, dq_ref, dkv_ref, across_ref, below_ref, above_ref, mine_ref):
    i = pl.program_id(0)
    t = head_terms(w_ref, dq_ref, dkv_ref)
    for n, ref in enumerate((across_ref, below_ref, above_ref, mine_ref)):

        @pl.when(i == n)
        def _(ref=ref):
            ref[...] = t.astype(ref.dtype)


def add_side(side_ref, top_ref, bottom_ref, out_ref):
    lo, hi = halves(side_ref)
    out_ref[lo, :] = (side_ref[lo, :].astype(f32) + top_ref[...].astype(f32)).astype(bf16)
    out_ref[hi, :] = (side_ref[hi, :].astype(f32) + bottom_ref[...].astype(f32)).astype(bf16)


def add_across(term_ref, down_ref, up_ref, out_ref):
    lo, hi = halves(term_ref)
    out_ref[lo, :] = (term_ref[lo, :].astype(f32) + up_ref[lo, :].astype(f32)).astype(bf16)
    out_ref[hi, :] = (term_ref[hi, :].astype(f32) + down_ref[hi, :].astype(f32)).astype(bf16)


def add_near(below_ref, above_ref, side_ref, down_ref, up_ref, out_b_ref, out_a_ref):
    lo, hi = halves(below_ref)
    more_b = side_ref[lo, :].astype(f32) + down_ref[lo, :].astype(f32)
    more_a = side_ref[hi, :].astype(f32) + up_ref[hi, :].astype(f32)
    out_b_ref[lo, :] = (below_ref[lo, :].astype(f32) + more_b).astype(bf16)
    out_b_ref[hi, :] = below_ref[hi, :]
    out_a_ref[lo, :] = above_ref[lo, :]
    out_a_ref[hi, :] = (above_ref[hi, :].astype(f32) + more_a).astype(bf16)


def add_last(mine_ref, a_ref, b_ref, c_ref, out_ref):
    got = a_ref[...].astype(f32) + b_ref[...].astype(f32) + c_ref[...].astype(f32)
    out_ref[...] = (mine_ref[...] + got).astype(bf16)


def with_table(kernel, us, grid, table, specs, args, outs, out_specs, scratch=()):
    return pl.pallas_call(
        kernel,
        out_shape=outs,
        grid_spec=pltpu.PrefetchScalarGridSpec(
            num_scalar_prefetch=1,
            grid=grid,
            in_specs=specs,
            out_specs=out_specs,
            scratch_shapes=list(scratch),
        ),
        compiler_params=pltpu.CompilerParams(vmem_limit_bytes=56 * 2**20),
        cost_estimate=cost(us),
    )(table, *args)


def scatter_tp(w_own, dq, dkv, table, beside):
    _, feats, cols = w_own.shape
    toks = dq.shape[1]
    sds = jax.ShapeDtypeStruct
    full, part = sds((feats, toks), bf16), sds((feats // 2, toks), bf16)

    def terms(kernel, us, first, count, outs, after=None):
        whole = lambda v: pl.BlockSpec(v.shape, lambda i, t: (0,) * len(v.shape))
        at = 1 + len(RELS) + first
        return with_table(
            kernel,
            us,
            (count,),
            table if after is None else tie((table,), after)[0],
            [
                pl.BlockSpec((1, feats, cols), lambda i, t: (t[at + i], 0, 0)),
                whole(dq),
                whole(dkv),
            ],
            (w_own, dq, dkv),
            outs,
            [whole(o) for o in outs],
        )

    top, bottom = terms(first_terms, 2.0, 0, 1, [part, part])
    extra = beside(top)
    top, bottom = y_step(top, -1), y_step(bottom, 1)
    side, down, up = terms(second_terms, 4.5, 1, 3, [full] * 3, extra)
    down, up = y_step(down, -1), y_step(up, 1)
    side = x_swap(call(add_side, full, 0.8)(side, top, bottom))
    mine = sds((feats, toks), f32)
    across, below, above, mine = terms(third_terms, 6.0, 4, 4, [full, full, full, mine])
    down, up, across, below, above = lax.optimization_barrier((down, up, across, below, above))
    across = x_swap(call(add_across, full, 0.8)(across, down, up))
    below, above = call(add_near, (full, full), 1.2)(below, above, side, down, up)
    below, above = y_step(below, -1), y_step(above, 1)
    return call(add_last, full, 1.5)(mine, across, below, above), extra


def join_kernel(place_ref, xa_ref, oa_ref, xb_ref, ob_ref, xc_ref, oc_ref, out_ref):
    step = pl.program_id(0)
    toks = oa_ref.shape[3]

    def put(x_ref, o_ref):
        for i in range(2):
            out_ref[0, i, 0, :, :toks] = x_ref[0, i, 0]
            out_ref[0, i, 0, :, toks:] = o_ref[0, i]

    pl.when(step < 4)(lambda: put(xa_ref, oa_ref))
    pl.when((step >= 4) & (step < 7))(lambda: put(xb_ref, ob_ref))
    pl.when(step == 7)(lambda: put(xc_ref, oc_ref))


def unrotate_norm(grad, raw, gain, cos, sin):
    top, bottom = grad[:HALF], grad[HALF:]
    d_normed = jnp.concatenate([top * cos + bottom * sin, bottom * cos - top * sin], axis=0)
    inv = lax.rsqrt(jnp.mean(raw * raw, axis=0, keepdims=True) + norm_eps)
    scaled = d_normed * gain
    along = jnp.mean(raw * scaled, axis=0, keepdims=True)
    return inv * scaled - raw * (inv * inv * inv * along)


def rotate_norm(raw, gain, cos, sin):
    inv = lax.rsqrt(jnp.mean(raw * raw, axis=0, keepdims=True) + norm_eps)
    normed = raw * inv * gain
    top, bottom = normed[:HALF], normed[HALF:]
    return jnp.concatenate([top * cos - bottom * sin, bottom * cos + top * sin], axis=0)


def heads_kernel(raw_ref, qg_ref, kg_ref, cos_ref, sin_ref, q_ref, kv_ref):
    cos, sin = cos_ref[...], sin_ref[...]
    for h in range(2):
        rows = slice(h * HD, (h + 1) * HD)
        q_ref[rows, :] = rotate_norm(raw_ref[rows, :], qg_ref[...], cos, sin).astype(bf16)
    kv_ref[0:HD, :] = rotate_norm(raw_ref[2 * HD : 3 * HD, :], kg_ref[...], cos, sin).astype(bf16)
    kv_ref[HD : 2 * HD, :] = raw_ref[3 * HD : 4 * HD, :].astype(bf16)


def attend_kernel(
    ctx_ref, q_ref, raw_ref, own_ref, m1_ref, m2_ref, go_ref, qg_ref, cos_ref, sin_ref,
    dq_ref, d_own_ref, d_m1_ref, d_m2_ref, e_s, dp_s, dk_s, dv_s,
):
    ctx = ctx_ref[0]
    toks = q_ref.shape[1]
    sub = 256
    cos, sin = cos_ref[...], sin_ref[...]
    blocks = (m2_ref, m1_ref, own_ref)
    for h in range(2):
        rows = slice(h * HD, (h + 1) * HD)
        q_t = q_ref[rows, :]
        q = q_t.T
        go = go_ref[:, rows]
        go_t = go.T
        total = jnp.zeros((1, toks), f32)
        weighted = jnp.zeros((1, toks), f32)
        for b in range(3):
            k = blocks[b][0:HD, :].T
            v = blocks[b][HD : 2 * HD, :].T
            for s0 in range(0, toks, sub):
                at = slice(b * toks + s0, b * toks + s0 + sub)
                s = jnp.dot(k[s0 : s0 + sub], q_t, preferred_element_type=f32) * query_scale
                dp = jnp.dot(v[s0 : s0 + sub], go_t, preferred_element_type=f32).astype(bf16)
                key = lax.broadcasted_iota(jnp.int32, (sub, toks), 0) + s0
                query = lax.broadcasted_iota(jnp.int32, (sub, toks), 1)
                if b == 0:
                    inside = (key > query) & (ctx >= 2)
                elif b == 1:
                    inside = (key >= 0) & (ctx >= 1)
                else:
                    inside = key <= query
                e = jnp.where(inside, jnp.exp(s), 0.0)
                e_s[at, :] = e
                dp_s[at, :] = dp
                total = total + jnp.sum(e, axis=0, keepdims=True)
                weighted = weighted + jnp.sum(e * dp.astype(f32), axis=0, keepdims=True)
        inv = 1.0 / total
        weighted = weighted * inv
        dq_t = jnp.zeros((HD, toks), f32)
        for b in range(3):
            for s0 in range(0, toks, sub):
                at = slice(b * toks + s0, b * toks + s0 + sub)
                p = e_s[at, :] * inv
                ds = (p * (dp_s[at, :].astype(f32) - weighted) * query_scale).astype(bf16)
                dv = jnp.dot(p.astype(bf16), go, preferred_element_type=f32)
                dk = jnp.dot(ds, q, preferred_element_type=f32)
                dq_t = dq_t + jnp.dot(
                    blocks[b][0:HD, s0 : s0 + sub], ds, preferred_element_type=f32
                )
                if h == 0:
                    dk_s[at, :] = dk
                    dv_s[at, :] = dv
                else:
                    out = (d_m2_ref, d_m1_ref, d_own_ref)[b]
                    out[0, s0 : s0 + sub, :] = (dk_s[at, :] + dk).astype(out.dtype)
                    out[1, s0 : s0 + sub, :] = (dv_s[at, :] + dv).astype(out.dtype)
        dq_low = dq_t.astype(bf16).astype(f32)
        dq_ref[rows, :] = unrotate_norm(dq_low, raw_ref[rows, :], qg_ref[...], cos, sin).astype(bf16)


def finish_kernel(own_ref, r1_ref, r2_ref, raw_ref, kg_ref, cos_ref, sin_ref, out_ref):
    def total(i):
        t = own_ref[i] + r1_ref[i].astype(f32) + r2_ref[i].astype(f32)
        return t.T.astype(bf16).astype(f32)

    out_ref[0:HD, :] = unrotate_norm(
        total(0), raw_ref[2 * HD : 3 * HD, :], kg_ref[...], cos_ref[...], sin_ref[...]
    ).astype(bf16)
    out_ref[HD : 2 * HD, :] = total(1).astype(bf16)


def shards(hidden_in, w_query, w_key, w_value, q_gain, k_gain, grad_out):
    toks, feats = hidden_in.shape
    sds = jax.ShapeDtypeStruct
    ctx = lax.axis_index("ctx")
    tp = lax.axis_index("tp")
    core, j = ctx % NC, ctx // NC
    xh, y = tp // NY, tp % NY
    n_tp = NXH * NY
    blk = feats // 4

    def owner(rel):
        return ((xh + rel[0]) % NXH) * NY + (y + rel[1]) % NY

    positions = ctx * toks + lax.iota(jnp.int32, toks)
    freqs = jnp.exp(-math.log(rope_base) * (2.0 * jnp.arange(HALF, dtype=f32) / HD))
    angles = freqs[:, None] * positions.astype(f32)[None, :]
    cos, sin = jnp.cos(angles), jnp.sin(angles)
    qg, kg = q_gain[:, None], k_gain[:, None]

    w_cat = jnp.concatenate([w_query, w_key, w_value], axis=1)
    w_own = w_cat.reshape(n_tp, feats, w_cat.shape[1])

    def project(total, parts, rels):
        for xs, rel in zip(parts, rels):
            ws = lax.dynamic_index_in_dim(w_own, owner(rel), 0, keepdims=False)
            term = lax.dot_general(ws, xs, (((0,), (0,)), ((), ())), preferred_element_type=f32)
            total = term if total is None else total + term
        return total

    begun = []

    def for_both(parts):
        x = jnp.stack(parts).reshape(len(parts), 2, NC, blk, toks)
        return x, lax.dynamic_index_in_dim(x, 1 - core, 2, keepdims=False)

    def beside(parts):
        begun.append(project(None, parts, RELS[:4]))
        begun.append(for_both(parts))
        return begun[0], *begun[1], cos, sin

    x_parts = gather_tp(hidden_in.T, beside)
    most = project(begun[0], x_parts[4:7], RELS[4:7])
    xb, ob = for_both(x_parts[4:7])
    last, most, xb, ob = lax.optimization_barrier((x_parts[7], most, xb, ob))
    raw = project(most, [last], RELS[7:])

    q_t, kv_t = call(heads_kernel, (sds((2 * HD, toks), bf16), sds((2 * HD, toks), bf16)), 1.5)(
        raw, qg, kg, cos, sin
    )
    rings = [[(a * NZ + z) * NC + c for z in range(NZ)] for a in range(NXL) for c in range(NC)]
    xl = j // NZ
    table = jnp.stack([core, *[owner(rel) for rel in RELS + SENT]]).astype(jnp.int32)

    def join(pairs, table):
        specs, first = [], 0
        for x, _ in pairs:
            at = lambda i, first=first, n=x.shape[0]: jnp.clip(i - first, 0, n - 1)
            first += x.shape[0]
            specs.append(
                pl.BlockSpec(
                    (1, 2, 1, blk, toks), lambda i, t, at=at: (at(i), 0, t[0], 0, 0)
                )
            )
            specs.append(pl.BlockSpec((1, 2, blk, toks), lambda i, t, at=at: (at(i), 0, 0, 0)))
        return with_table(
            join_kernel,
            6.0,
            (n_tp,),
            table,
            specs,
            [v for pair in pairs for v in pair],
            jax.ShapeDtypeStruct((NY, 2, NXH, blk, 2 * toks), bf16),
            pl.BlockSpec(
                (1, 2, 1, blk, 2 * toks), lambda i, t: (t[i + 1] % NY, 0, t[i + 1] // NY, 0, 0)
            ),
        ).reshape(NZ, NXL * blk, 2 * toks)

    def along_z(g):
        return lax.psum_scatter(
            g, "ctx", scatter_dimension=0, tiled=True, axis_index_groups=rings
        )[0]

    def across_x(g):
        g = g.reshape(NXL, blk, -1)
        keep = lax.dynamic_index_in_dim(g, xl, 0, keepdims=False)
        send = lax.dynamic_index_in_dim(g, 1 - xl, 0, keepdims=False)
        outs = [sds((blk, w), f32) for w in (2 * HD, HD, HD)]
        return call(add_pair, outs, 0.7)(keep, xlo_swap(send))

    kv1 = from_behind(kv_t, 1)
    kv2 = from_behind(kv_t, 2)
    xa, oa = begun[1]
    xc, oc = for_both([last])
    pairs = [(xa, core_swap(oa)), (xb, core_swap(ob)), (xc, core_swap(oc))]
    pair = sds((2, toks, HD), bf16)
    dq_raw, d_own, d1, d2 = call(
        attend_kernel,
        (sds((2 * HD, toks), bf16), sds((2, toks, HD), f32), pair, pair),
        5.5,
        (
            pltpu.VMEM((3 * toks, toks), f32),
            pltpu.VMEM((3 * toks, toks), bf16),
            pltpu.VMEM((3 * toks, HD), f32),
            pltpu.VMEM((3 * toks, HD), f32),
        ),
        smem_first=True,
    )(ctx[None], q_t, raw, kv_t, kv1, kv2, grad_out, qg, cos, sin)
    r1 = from_behind(d1, -1)
    r2 = from_behind(d2, -2)
    x_pair = join(pairs, tie((table,), dq_raw)[0])
    dq_other = core_swap(dq_raw)
    r1, r2, x_pair, dq_other = lax.optimization_barrier((r1, r2, x_pair, dq_other))
    dkv_raw = call(finish_kernel, sds((2 * HD, toks), bf16), 1.3)(
        d_own, r1, r2, raw, kg, cos, sin
    )
    dkv_other = core_swap(dkv_raw)

    def beside_tail(after):
        here, there, _ = lax.optimization_barrier((dkv_raw, dkv_other, after))
        d_pair = jnp.concatenate(
            [
                jnp.concatenate([dq_raw, dq_other], axis=1),
                jnp.concatenate([here, there], axis=1),
            ]
        )
        g = lax.dot_general(x_pair, d_pair, (((2,), (1,)), ((), ())), preferred_element_type=f32)
        return g.astype(bf16)

    grad_input, g = scatter_tp(w_own, dq_raw, dkv_raw, table, beside_tail)
    grad_input = grad_input.T
    grad_w = across_x(along_z(g))
    return (grad_input, *grad_w)


def solution(mesh):
    placed = (P("ctx", "tp"), P(None, "tp"), P(None, "tp"), P(None, "tp"), P(), P(), P("ctx", "tp"))
    return jax.shard_map(
        shards,
        mesh=mesh,
        in_specs=placed,
        out_specs=(P("ctx", "tp"), P("ctx", "tp"), P("ctx", "tp"), P("ctx", "tp")),
        check_vma=False,
    )
```

```python
import functools
import math

import jax
import jax.numpy as jnp
from jax import lax
from jax.experimental import pallas as pl
from jax.experimental.pallas import tpu as pltpu
from jax.sharding import PartitionSpec as P

WINDOW = 1024
HD = 128
HALF = 64
NY, NXH = 4, 2
NXL, NZ, NC = 2, 8, 2

query_scale = 1.0 / math.sqrt(168.0)
rope_base = 10000.0
norm_eps = 1e-06
f32 = jnp.float32
bf16 = jnp.bfloat16
VMEM = pl.BlockSpec(memory_space=pltpu.VMEM)


def tp_perm(dx, dy):
    return [
        (x * NY + y, ((x + dx) % NXH) * NY + (y + dy) % NY)
        for x in range(NXH)
        for y in range(NY)
    ]


def y_step(v, d):
    return lax.ppermute(v, "tp", tp_perm(0, d))


def x_swap(v):
    return lax.ppermute(v, "tp", tp_perm(1, 0))


def core_swap(v):
    return lax.ppermute(v, "ctx", [(i, i ^ 1) for i in range(NXL * NZ * NC)])


def xlo_swap(v):
    n = NXL * NZ * NC
    return lax.ppermute(v, "ctx", [(i, (i + n // 2) % n) for i in range(n)])


def from_behind(block, distance):
    n = NXL * NZ * NC
    route = [(i - distance, i) for i in range(n) if 0 <= i - distance < n]
    return lax.ppermute(block, "ctx", route)


def tie(values, *after):
    return lax.optimization_barrier((*values, *after))[: len(values)]


RELS = [(0, 0), (0, 3), (0, 1), (1, 0), (0, 2), (1, 3), (1, 1), (1, 2)]
SENT = [(1, 2), (0, 2), (1, 3), (1, 1), (1, 0), (0, 3), (0, 1), (0, 0)]


def gather_tp(own, beside_second):
    half = own.shape[0] // 2
    below = y_step(own, 1)
    above = y_step(own, -1)
    across = x_swap(own)
    second = (
        jnp.concatenate([below[:half], across[half:]]),
        jnp.concatenate([across[:half], above[half:]]),
        jnp.concatenate([below[:half], above[half:]]),
    )
    up = y_step(second[0], 1)
    down = y_step(second[1], -1)
    side = x_swap(second[2])
    far = jnp.concatenate([up[:half], down[half:]])
    x_below = jnp.concatenate([side[:half], up[half:]])
    x_above = jnp.concatenate([down[:half], side[half:]])
    third = tie((side[:half], side[half:]), *beside_second([own, below, above, across]))
    far_up = y_step(third[0], 1)
    far_down = y_step(third[1], -1)
    x_far = jnp.concatenate([far_up, far_down])
    return [own, below, above, across, far, x_below, x_above, x_far]


def cost(us):
    return pl.CostEstimate(flops=0, bytes_accessed=int(us * 3.4e6), transcendentals=0)


def call(kernel, outs, us, scratch=(), smem_first=False, mib=40):
    def run(*args):
        in_specs = [VMEM] * len(args)
        if smem_first:
            in_specs[0] = pl.BlockSpec(memory_space=pltpu.SMEM)
        return pl.pallas_call(
            kernel,
            out_shape=outs,
            in_specs=in_specs,
            out_specs=jax.tree.map(lambda _: VMEM, outs),
            scratch_shapes=list(scratch),
            compiler_params=pltpu.CompilerParams(vmem_limit_bytes=mib * 2**20),
            cost_estimate=cost(us),
        )(*args)

    return run


def halves(ref):
    half = ref.shape[-2] // 2
    return slice(0, half), slice(half, 2 * half)


def add_pair(keep_ref, got_ref, q_ref, k_ref, v_ref):
    total = keep_ref[...].astype(f32) + got_ref[...].astype(f32)
    q_ref[...] = total[:, : 2 * HD]
    k_ref[...] = total[:, 2 * HD : 3 * HD]
    v_ref[...] = total[:, 3 * HD :]


def head_terms(w_ref, dq_ref, dkv_ref):
    width = dq_ref.shape[0]
    t = jnp.dot(w_ref[0, :, :width], dq_ref[...], preferred_element_type=f32)
    return t + jnp.dot(w_ref[0, :, width:], dkv_ref[...], preferred_element_type=f32)


def first_terms(own_ref, w_ref, dq_ref, dkv_ref, top_ref, bottom_ref):
    t = head_terms(w_ref, dq_ref, dkv_ref).astype(bf16)
    lo, hi = halves(w_ref)
    top_ref[...] = t[lo]
    bottom_ref[...] = t[hi]


def second_terms(own_ref, w_ref, dq_ref, dkv_ref, side_ref, down_ref, up_ref):
    lo, hi = halves(w_ref)
    i = pl.program_id(0)
    t = head_terms(w_ref, dq_ref, dkv_ref).astype(bf16)

    @pl.when(i == 0)
    def _():
        down_ref[lo, :] = t[lo]
        up_ref[hi, :] = t[hi]

    @pl.when(i == 1)
    def _():
        side_ref[lo, :] = t[lo]
        down_ref[hi, :] = t[hi]

    @pl.when(i == 2)
    def _():
        up_ref[lo, :] = t[lo]
        side_ref[hi, :] = t[hi]


def third_terms(own_ref, w_ref, dq_ref, dkv_ref, across_ref, below_ref, above_ref, mine_ref):
    i = pl.program_id(0)
    t = head_terms(w_ref, dq_ref, dkv_ref)
    for n, ref in enumerate((across_ref, below_ref, above_ref, mine_ref)):

        @pl.when(i == n)
        def _(ref=ref):
            ref[...] = t.astype(ref.dtype)


def add_side(side_ref, top_ref, bottom_ref, out_ref):
    lo, hi = halves(side_ref)
    out_ref[lo, :] = (side_ref[lo, :].astype(f32) + top_ref[...].astype(f32)).astype(bf16)
    out_ref[hi, :] = (side_ref[hi, :].astype(f32) + bottom_ref[...].astype(f32)).astype(bf16)


def add_across(term_ref, down_ref, up_ref, out_ref):
    lo, hi = halves(term_ref)
    out_ref[lo, :] = (term_ref[lo, :].astype(f32) + up_ref[lo, :].astype(f32)).astype(bf16)
    out_ref[hi, :] = (term_ref[hi, :].astype(f32) + down_ref[hi, :].astype(f32)).astype(bf16)


def add_near(below_ref, above_ref, side_ref, down_ref, up_ref, out_b_ref, out_a_ref):
    lo, hi = halves(below_ref)
    more_b = side_ref[lo, :].astype(f32) + down_ref[lo, :].astype(f32)
    more_a = side_ref[hi, :].astype(f32) + up_ref[hi, :].astype(f32)
    out_b_ref[lo, :] = (below_ref[lo, :].astype(f32) + more_b).astype(bf16)
    out_b_ref[hi, :] = below_ref[hi, :]
    out_a_ref[lo, :] = above_ref[lo, :]
    out_a_ref[hi, :] = (above_ref[hi, :].astype(f32) + more_a).astype(bf16)


def add_last(mine_ref, a_ref, b_ref, c_ref, out_ref):
    got = a_ref[...].astype(f32) + b_ref[...].astype(f32) + c_ref[...].astype(f32)
    out_ref[...] = (mine_ref[...] + got).astype(bf16)


def with_table(kernel, us, grid, table, specs, args, outs, out_specs, scratch=(), alias={}):
    return pl.pallas_call(
        kernel,
        out_shape=outs,
        grid_spec=pltpu.PrefetchScalarGridSpec(
            num_scalar_prefetch=1,
            grid=grid,
            in_specs=specs,
            out_specs=out_specs,
            scratch_shapes=list(scratch),
        ),
        compiler_params=pltpu.CompilerParams(vmem_limit_bytes=56 * 2**20),
        cost_estimate=cost(us),
        input_output_aliases=alias,
    )(table, *args)


def scatter_tp(w_own, dq, dkv, table, beside):
    _, feats, cols = w_own.shape
    toks = dq.shape[1]
    sds = jax.ShapeDtypeStruct
    full, part = sds((feats, toks), bf16), sds((feats // 2, toks), bf16)

    def terms(kernel, us, first, count, outs, after=None):
        whole = lambda v: pl.BlockSpec(v.shape, lambda i, t: (0,) * len(v.shape))
        at = 1 + len(RELS) + first
        return with_table(
            kernel,
            us,
            (count,),
            table if after is None else tie((table,), after)[0],
            [
                pl.BlockSpec((1, feats, cols), lambda i, t: (t[at + i], 0, 0)),
                whole(dq),
                whole(dkv),
            ],
            (w_own, dq, dkv),
            outs,
            [whole(o) for o in outs],
        )

    top, bottom = terms(first_terms, 2.0, 0, 1, [part, part])
    extra = beside(top)
    top, bottom = y_step(top, -1), y_step(bottom, 1)
    side, down, up = terms(second_terms, 4.5, 1, 3, [full] * 3, extra)
    down, up = y_step(down, -1), y_step(up, 1)
    side = x_swap(call(add_side, full, 0.8)(side, top, bottom))
    mine = sds((feats, toks), f32)
    across, below, above, mine = terms(third_terms, 6.0, 4, 4, [full, full, full, mine])
    down, up, across, below, above = lax.optimization_barrier((down, up, across, below, above))
    across = x_swap(call(add_across, full, 0.8)(across, down, up))
    below, above = call(add_near, (full, full), 1.2)(below, above, side, down, up)
    below, above = y_step(below, -1), y_step(above, 1)
    return call(add_last, full, 1.5)(mine, across, below, above), extra


def join_first(table_ref, x_ref, o_ref, out_ref):
    toks = o_ref.shape[3]
    for i in range(2):
        out_ref[0, i, 0, :, :toks] = x_ref[0, i, 0]
        out_ref[0, i, 0, :, toks:] = o_ref[0, i]


def join_rest(table_ref, xb_ref, ob_ref, xc_ref, oc_ref, begun_ref, out_ref):
    step = pl.program_id(0)
    pl.when(step < 3)(lambda: join_first(table_ref, xb_ref, ob_ref, out_ref))
    pl.when(step == 3)(lambda: join_first(table_ref, xc_ref, oc_ref, out_ref))


def unrotate_norm(grad, raw, gain, cos, sin):
    top, bottom = grad[:HALF], grad[HALF:]
    d_normed = jnp.concatenate([top * cos + bottom * sin, bottom * cos - top * sin], axis=0)
    inv = lax.rsqrt(jnp.mean(raw * raw, axis=0, keepdims=True) + norm_eps)
    scaled = d_normed * gain
    along = jnp.mean(raw * scaled, axis=0, keepdims=True)
    return inv * scaled - raw * (inv * inv * inv * along)


def rotate_norm(raw, gain, cos, sin):
    inv = lax.rsqrt(jnp.mean(raw * raw, axis=0, keepdims=True) + norm_eps)
    normed = raw * inv * gain
    top, bottom = normed[:HALF], normed[HALF:]
    return jnp.concatenate([top * cos - bottom * sin, bottom * cos + top * sin], axis=0)


def heads_kernel(
    most_ref, w_ref, last_ref, qg_ref, kg_ref, cos_ref, sin_ref, q_ref, kv_ref, raw_ref
):
    cos, sin = cos_ref[...], sin_ref[...]
    raw_ref[...] = most_ref[...] + jnp.dot(
        w_ref[...], last_ref[...], preferred_element_type=f32
    )
    for h in range(2):
        rows = slice(h * HD, (h + 1) * HD)
        q_ref[rows, :] = rotate_norm(raw_ref[rows, :], qg_ref[...], cos, sin).astype(bf16)
    kv_ref[0:HD, :] = rotate_norm(raw_ref[2 * HD : 3 * HD, :], kg_ref[...], cos, sin).astype(bf16)
    kv_ref[HD : 2 * HD, :] = raw_ref[3 * HD : 4 * HD, :].astype(bf16)


def attend_kernel(
    ctx_ref, q_ref, raw_ref, own_ref, m1_ref, m2_ref, go_ref, qg_ref, cos_ref, sin_ref,
    dq_ref, d_own_ref, d_m1_ref, d_m2_ref, e_s, dp_s, dk_s, dv_s,
):
    ctx = ctx_ref[0]
    toks = q_ref.shape[1]
    sub = 256
    cos, sin = cos_ref[...], sin_ref[...]
    blocks = (m2_ref, m1_ref, own_ref)
    for h in range(2):
        rows = slice(h * HD, (h + 1) * HD)
        q_t = q_ref[rows, :]
        q = q_t.T
        go = go_ref[:, rows]
        go_t = go.T
        total = jnp.zeros((1, toks), f32)
        weighted = jnp.zeros((1, toks), f32)
        for b in range(3):
            k = blocks[b][0:HD, :].T
            v = blocks[b][HD : 2 * HD, :].T
            for s0 in range(0, toks, sub):
                at = slice(b * toks + s0, b * toks + s0 + sub)
                s = jnp.dot(k[s0 : s0 + sub], q_t, preferred_element_type=f32) * query_scale
                dp = jnp.dot(v[s0 : s0 + sub], go_t, preferred_element_type=f32).astype(bf16)
                key = lax.broadcasted_iota(jnp.int32, (sub, toks), 0) + s0
                query = lax.broadcasted_iota(jnp.int32, (sub, toks), 1)
                if b == 0:
                    inside = (key > query) & (ctx >= 2)
                elif b == 1:
                    inside = (key >= 0) & (ctx >= 1)
                else:
                    inside = key <= query
                e = jnp.where(inside, jnp.exp(s), 0.0)
                e_s[at, :] = e
                dp_s[at, :] = dp
                total = total + jnp.sum(e, axis=0, keepdims=True)
                weighted = weighted + jnp.sum(e * dp.astype(f32), axis=0, keepdims=True)
        inv = 1.0 / total
        weighted = weighted * inv
        dq_t = jnp.zeros((HD, toks), f32)
        for b in range(3):
            for s0 in range(0, toks, sub):
                at = slice(b * toks + s0, b * toks + s0 + sub)
                p = e_s[at, :] * inv
                ds = (p * (dp_s[at, :].astype(f32) - weighted) * query_scale).astype(bf16)
                dv = jnp.dot(p.astype(bf16), go, preferred_element_type=f32)
                dk = jnp.dot(ds, q, preferred_element_type=f32)
                dq_t = dq_t + jnp.dot(
                    blocks[b][0:HD, s0 : s0 + sub], ds, preferred_element_type=f32
                )
                if h == 0:
                    dk_s[at, :] = dk
                    dv_s[at, :] = dv
                else:
                    out = (d_m2_ref, d_m1_ref, d_own_ref)[b]
                    out[0, s0 : s0 + sub, :] = (dk_s[at, :] + dk).astype(out.dtype)
                    out[1, s0 : s0 + sub, :] = (dv_s[at, :] + dv).astype(out.dtype)
        dq_low = dq_t.astype(bf16).astype(f32)
        dq_ref[rows, :] = unrotate_norm(dq_low, raw_ref[rows, :], qg_ref[...], cos, sin).astype(bf16)


def finish_kernel(own_ref, r1_ref, r2_ref, raw_ref, kg_ref, cos_ref, sin_ref, out_ref):
    def total(i):
        t = own_ref[i] + r1_ref[i].astype(f32) + r2_ref[i].astype(f32)
        return t.T.astype(bf16).astype(f32)

    out_ref[0:HD, :] = unrotate_norm(
        total(0), raw_ref[2 * HD : 3 * HD, :], kg_ref[...], cos_ref[...], sin_ref[...]
    ).astype(bf16)
    out_ref[HD : 2 * HD, :] = total(1).astype(bf16)


def shards(hidden_in, w_query, w_key, w_value, q_gain, k_gain, grad_out):
    toks, feats = hidden_in.shape
    sds = jax.ShapeDtypeStruct
    ctx = lax.axis_index("ctx")
    tp = lax.axis_index("tp")
    core, j = ctx % NC, ctx // NC
    xh, y = tp // NY, tp % NY
    n_tp = NXH * NY
    blk = feats // 4

    def owner(rel):
        return ((xh + rel[0]) % NXH) * NY + (y + rel[1]) % NY

    positions = ctx * toks + lax.iota(jnp.int32, toks)
    freqs = jnp.exp(-math.log(rope_base) * (2.0 * jnp.arange(HALF, dtype=f32) / HD))
    angles = freqs[:, None] * positions.astype(f32)[None, :]
    cos, sin = jnp.cos(angles), jnp.sin(angles)
    qg, kg = q_gain[:, None], k_gain[:, None]

    w_cat = jnp.concatenate([w_query, w_key, w_value], axis=1)
    w_own = w_cat.reshape(n_tp, feats, w_cat.shape[1])

    table = jnp.stack([core, *[owner(rel) for rel in RELS + SENT]]).astype(jnp.int32)
    w_last = lax.dynamic_index_in_dim(w_own, owner(RELS[7]), 0, keepdims=False).T

    def project(total, parts, rels):
        for xs, rel in zip(parts, rels):
            ws = lax.dynamic_index_in_dim(w_own, owner(rel), 0, keepdims=False)
            term = lax.dot_general(ws, xs, (((0,), (0,)), ((), ())), preferred_element_type=f32)
            total = term if total is None else total + term
        return total

    begun = []

    def for_both(parts):
        x = jnp.stack(parts).reshape(len(parts), 2, NC, blk, toks)
        return x, lax.dynamic_index_in_dim(x, 1 - core, 2, keepdims=False)

    def beside(parts):
        begun.append(project(None, parts, RELS[:4]))
        begun.append(for_both(parts))
        return begun[0], *begun[1], cos, sin, w_last, table

    x_parts = gather_tp(hidden_in.T, beside)
    most = project(begun[0], x_parts[4:7], RELS[4:7])
    xb, ob = for_both(x_parts[4:7])
    last, most, xb, ob = lax.optimization_barrier((x_parts[7], most, xb, ob))

    low = sds((2 * HD, toks), bf16)
    q_t, kv_t, raw = call(heads_kernel, (low, low, sds(most.shape, f32)), 2.5)(
        most, w_last, last, qg, kg, cos, sin
    )
    rings = [[(a * NZ + z) * NC + c for z in range(NZ)] for a in range(NXL) for c in range(NC)]
    xl = j // NZ

    def x_specs(at):
        return [
            pl.BlockSpec((1, 2, 1, blk, toks), lambda i, t: (at(i), 0, t[0], 0, 0)),
            pl.BlockSpec((1, 2, blk, toks), lambda i, t: (at(i), 0, 0, 0)),
        ]

    def pair_spec(first):
        return pl.BlockSpec(
            (1, 2, 1, blk, 2 * toks),
            lambda i, t: (t[first + i] % NY, 0, t[first + i] // NY, 0, 0),
        )

    pair_shape = sds((NY, 2, NXH, blk, 2 * toks), bf16)

    def along_z(g):
        return lax.psum_scatter(
            g, "ctx", scatter_dimension=0, tiled=True, axis_index_groups=rings
        )[0]

    def across_x(g):
        g = g.reshape(NXL, blk, -1)
        keep = lax.dynamic_index_in_dim(g, xl, 0, keepdims=False)
        send = lax.dynamic_index_in_dim(g, 1 - xl, 0, keepdims=False)
        outs = [sds((blk, w), f32) for w in (2 * HD, HD, HD)]
        return call(add_pair, outs, 0.7)(keep, xlo_swap(send))

    kv1 = from_behind(kv_t, 1)
    kv2 = from_behind(kv_t, 2)
    xa, oa = begun[1]
    joined = with_table(
        join_first,
        4.0,
        (4,),
        tie((table,), kv_t)[0],
        x_specs(lambda i: i),
        (xa, core_swap(oa)),
        pair_shape,
        pair_spec(1),
    )
    kv2, joined = lax.optimization_barrier((kv2, joined))
    xc, oc = for_both(tie((last,), kv_t))
    pair = sds((2, toks, HD), bf16)
    dq_raw, d_own, d1, d2 = call(
        attend_kernel,
        (sds((2 * HD, toks), bf16), sds((2, toks, HD), f32), pair, pair),
        5.5,
        (
            pltpu.VMEM((3 * toks, toks), f32),
            pltpu.VMEM((3 * toks, toks), bf16),
            pltpu.VMEM((3 * toks, HD), f32),
            pltpu.VMEM((3 * toks, HD), f32),
        ),
        smem_first=True,
    )(ctx[None], q_t, raw, kv_t, kv1, kv2, grad_out, qg, cos, sin)
    r1 = from_behind(d1, -1)
    r2 = from_behind(d2, -2)
    x_pair = with_table(
        join_rest,
        4.0,
        (4,),
        tie((table,), dq_raw)[0],
        [
            *x_specs(lambda i: jnp.minimum(i, 2)),
            *x_specs(lambda i: 0),
            pl.BlockSpec(memory_space=pl.ANY),
        ],
        (xb, core_swap(ob), xc, core_swap(oc), joined),
        pair_shape,
        pair_spec(5),
        alias={5: 0},
    ).reshape(NZ, NXL * blk, 2 * toks)
    dq_other = core_swap(dq_raw)
    dq_pair = jnp.concatenate([dq_raw, dq_other], axis=1)
    r1, r2, x_pair, dq_pair = lax.optimization_barrier((r1, r2, x_pair, dq_pair))
    dkv_raw = call(finish_kernel, sds((2 * HD, toks), bf16), 1.3)(
        d_own, r1, r2, raw, kg, cos, sin
    )
    dkv_other = core_swap(dkv_raw)

    def beside_tail(after):
        here, there, _ = lax.optimization_barrier((dkv_raw, dkv_other, after))
        d_pair = jnp.concatenate([dq_pair, jnp.concatenate([here, there], axis=1)])
        g = lax.dot_general(x_pair, d_pair, (((2,), (1,)), ((), ())), preferred_element_type=f32)
        return g.astype(bf16)

    grad_input, g = scatter_tp(w_own, dq_raw, dkv_raw, table, beside_tail)
    grad_input = grad_input.T
    grad_w = across_x(along_z(g))
    return (grad_input, *grad_w)


def solution(mesh):
    placed = (P("ctx", "tp"), P(None, "tp"), P(None, "tp"), P(None, "tp"), P(), P(), P("ctx", "tp"))
    return jax.shard_map(
        shards,
        mesh=mesh,
        in_specs=placed,
        out_specs=(P("ctx", "tp"), P("ctx", "tp"), P("ctx", "tp"), P("ctx", "tp")),
        check_vma=False,
    )
```

```python
import functools
import math

import jax
import jax.numpy as jnp
from jax import lax
from jax.experimental import pallas as pl
from jax.experimental.pallas import tpu as pltpu
from jax.sharding import PartitionSpec as P

WINDOW = 1024
HD = 128
HALF = 64
NY, NXH = 4, 2
NXL, NZ, NC = 2, 8, 2

query_scale = 1.0 / math.sqrt(168.0)
rope_base = 10000.0
norm_eps = 1e-06
f32 = jnp.float32
bf16 = jnp.bfloat16
VMEM = pl.BlockSpec(memory_space=pltpu.VMEM)


def tp_perm(dx, dy):
    return [
        (x * NY + y, ((x + dx) % NXH) * NY + (y + dy) % NY)
        for x in range(NXH)
        for y in range(NY)
    ]


def y_step(v, d):
    return lax.ppermute(v, "tp", tp_perm(0, d))


def x_swap(v):
    return lax.ppermute(v, "tp", tp_perm(1, 0))


def core_swap(v):
    return lax.ppermute(v, "ctx", [(i, i ^ 1) for i in range(NXL * NZ * NC)])


def xlo_swap(v):
    n = NXL * NZ * NC
    return lax.ppermute(v, "ctx", [(i, (i + n // 2) % n) for i in range(n)])


def from_behind(block, distance):
    n = NXL * NZ * NC
    route = [(i - distance, i) for i in range(n) if 0 <= i - distance < n]
    return lax.ppermute(block, "ctx", route)


def tie(values, *after):
    return lax.optimization_barrier((*values, *after))[: len(values)]


RELS = [(0, 0), (0, 3), (0, 1), (1, 0), (0, 2), (1, 3), (1, 1), (1, 2)]
SENT = [(1, 2), (0, 2), (1, 3), (1, 1), (1, 0), (0, 3), (0, 1), (0, 0)]


def gather_tp(own, beside_second):
    half = own.shape[0] // 2
    below = y_step(own, 1)
    above = y_step(own, -1)
    across = x_swap(own)
    second = (
        jnp.concatenate([below[:half], across[half:]]),
        jnp.concatenate([across[:half], above[half:]]),
        jnp.concatenate([below[:half], above[half:]]),
    )
    up = y_step(second[0], 1)
    down = y_step(second[1], -1)
    side = x_swap(second[2])
    far = jnp.concatenate([up[:half], down[half:]])
    x_below = jnp.concatenate([side[:half], up[half:]])
    x_above = jnp.concatenate([down[:half], side[half:]])
    third = tie((side[:half], side[half:]), *beside_second([own, below, above, across]))
    far_up = y_step(third[0], 1)
    far_down = y_step(third[1], -1)
    x_far = jnp.concatenate([far_up, far_down])
    return [own, below, above, across, far, x_below, x_above, x_far]


def cost(us):
    return pl.CostEstimate(flops=0, bytes_accessed=int(us * 3.4e6), transcendentals=0)


def call(kernel, outs, us, scratch=(), smem_first=False, mib=40):
    def run(*args):
        in_specs = [VMEM] * len(args)
        if smem_first:
            in_specs[0] = pl.BlockSpec(memory_space=pltpu.SMEM)
        return pl.pallas_call(
            kernel,
            out_shape=outs,
            in_specs=in_specs,
            out_specs=jax.tree.map(lambda _: VMEM, outs),
            scratch_shapes=list(scratch),
            compiler_params=pltpu.CompilerParams(vmem_limit_bytes=mib * 2**20),
            cost_estimate=cost(us),
        )(*args)

    return run


def halves(ref):
    half = ref.shape[-2] // 2
    return slice(0, half), slice(half, 2 * half)


def add_pair(keep_ref, got_ref, q_ref, k_ref, v_ref):
    total = keep_ref[...].astype(f32) + got_ref[...].astype(f32)
    q_ref[...] = total[:, : 2 * HD]
    k_ref[...] = total[:, 2 * HD : 3 * HD]
    v_ref[...] = total[:, 3 * HD :]


def first_terms(own_ref, w_ref, d_ref, top_ref, bottom_ref):
    t = jnp.dot(w_ref[0], d_ref[...], preferred_element_type=f32).astype(bf16)
    lo, hi = halves(w_ref)
    top_ref[...] = t[lo]
    bottom_ref[...] = t[hi]


def second_terms(own_ref, w_ref, d_ref, side_ref, down_ref, up_ref):
    lo, hi = halves(w_ref)
    i = pl.program_id(0)
    t = jnp.dot(w_ref[0], d_ref[...], preferred_element_type=f32).astype(bf16)

    @pl.when(i == 0)
    def _():
        down_ref[lo, :] = t[lo]
        up_ref[hi, :] = t[hi]

    @pl.when(i == 1)
    def _():
        side_ref[lo, :] = t[lo]
        down_ref[hi, :] = t[hi]

    @pl.when(i == 2)
    def _():
        up_ref[lo, :] = t[lo]
        side_ref[hi, :] = t[hi]


def third_terms(own_ref, w_ref, d_ref, across_ref, below_ref, above_ref, mine_ref):
    i = pl.program_id(0)
    t = jnp.dot(w_ref[0], d_ref[...], preferred_element_type=f32)
    for n, ref in enumerate((across_ref, below_ref, above_ref, mine_ref)):

        @pl.when(i == n)
        def _(ref=ref):
            ref[...] = t.astype(ref.dtype)


def add_side(side_ref, top_ref, bottom_ref, out_ref):
    lo, hi = halves(side_ref)
    out_ref[lo, :] = (side_ref[lo, :].astype(f32) + top_ref[...].astype(f32)).astype(bf16)
    out_ref[hi, :] = (side_ref[hi, :].astype(f32) + bottom_ref[...].astype(f32)).astype(bf16)


def add_across(term_ref, down_ref, up_ref, out_ref):
    lo, hi = halves(term_ref)
    out_ref[lo, :] = (term_ref[lo, :].astype(f32) + up_ref[lo, :].astype(f32)).astype(bf16)
    out_ref[hi, :] = (term_ref[hi, :].astype(f32) + down_ref[hi, :].astype(f32)).astype(bf16)


def add_near(below_ref, above_ref, side_ref, down_ref, up_ref, out_b_ref, out_a_ref):
    lo, hi = halves(below_ref)
    more_b = side_ref[lo, :].astype(f32) + down_ref[lo, :].astype(f32)
    more_a = side_ref[hi, :].astype(f32) + up_ref[hi, :].astype(f32)
    out_b_ref[lo, :] = (below_ref[lo, :].astype(f32) + more_b).astype(bf16)
    out_b_ref[hi, :] = below_ref[hi, :]
    out_a_ref[lo, :] = above_ref[lo, :]
    out_a_ref[hi, :] = (above_ref[hi, :].astype(f32) + more_a).astype(bf16)


def add_last(mine_ref, a_ref, b_ref, c_ref, out_ref):
    got = a_ref[...].astype(f32) + b_ref[...].astype(f32) + c_ref[...].astype(f32)
    out_ref[...] = (mine_ref[...] + got).astype(bf16)


def with_table(kernel, us, grid, table, specs, args, outs, out_specs, scratch=(), alias={}):
    return pl.pallas_call(
        kernel,
        out_shape=outs,
        grid_spec=pltpu.PrefetchScalarGridSpec(
            num_scalar_prefetch=1,
            grid=grid,
            in_specs=specs,
            out_specs=out_specs,
            scratch_shapes=list(scratch),
        ),
        compiler_params=pltpu.CompilerParams(vmem_limit_bytes=56 * 2**20),
        cost_estimate=cost(us),
        input_output_aliases=alias,
    )(table, *args)


def scatter_tp(w_own, d_all, table, beside):
    _, feats, cols = w_own.shape
    toks = d_all.shape[1]
    sds = jax.ShapeDtypeStruct
    full, part = sds((feats, toks), bf16), sds((feats // 2, toks), bf16)

    def terms(kernel, us, first, count, outs, after=None):
        whole = lambda v: pl.BlockSpec(v.shape, lambda i, t: (0,) * len(v.shape))
        at = 1 + len(RELS) + first
        return with_table(
            kernel,
            us,
            (count,),
            table if after is None else tie((table,), after)[0],
            [
                pl.BlockSpec((1, feats, cols), lambda i, t: (t[at + i], 0, 0)),
                whole(d_all),
            ],
            (w_own, d_all),
            outs,
            [whole(o) for o in outs],
        )

    top, bottom = terms(first_terms, 2.0, 0, 1, [part, part])
    extra = beside(top)
    top, bottom = y_step(top, -1), y_step(bottom, 1)
    side, down, up = terms(second_terms, 4.5, 1, 3, [full] * 3, extra)
    down, up = y_step(down, -1), y_step(up, 1)
    side = x_swap(call(add_side, full, 0.8)(side, top, bottom))
    mine = sds((feats, toks), f32)
    across, below, above, mine = terms(third_terms, 6.0, 4, 4, [full, full, full, mine])
    down, up, across, below, above = lax.optimization_barrier((down, up, across, below, above))
    across = x_swap(call(add_across, full, 0.8)(across, down, up))
    below, above = call(add_near, (full, full), 1.2)(below, above, side, down, up)
    below, above = y_step(below, -1), y_step(above, 1)
    return call(add_last, full, 1.5)(mine, across, below, above), extra


def join_first(table_ref, x_ref, o_ref, out_ref):
    toks = o_ref.shape[3]
    for i in range(2):
        out_ref[0, i, 0, :, :toks] = x_ref[0, i, 0]
        out_ref[0, i, 0, :, toks:] = o_ref[0, i]


def join_rest(table_ref, xb_ref, ob_ref, xc_ref, oc_ref, begun_ref, out_ref):
    step = pl.program_id(0)
    pl.when(step < 3)(lambda: join_first(table_ref, xb_ref, ob_ref, out_ref))
    pl.when(step == 3)(lambda: join_first(table_ref, xc_ref, oc_ref, out_ref))


def unrotate_norm(grad, raw, gain, cos, sin):
    top, bottom = grad[:HALF], grad[HALF:]
    d_normed = jnp.concatenate([top * cos + bottom * sin, bottom * cos - top * sin], axis=0)
    inv = lax.rsqrt(jnp.mean(raw * raw, axis=0, keepdims=True) + norm_eps)
    scaled = d_normed * gain
    along = jnp.mean(raw * scaled, axis=0, keepdims=True)
    return inv * scaled - raw * (inv * inv * inv * along)


def rotate_norm(raw, gain, cos, sin):
    inv = lax.rsqrt(jnp.mean(raw * raw, axis=0, keepdims=True) + norm_eps)
    normed = raw * inv * gain
    top, bottom = normed[:HALF], normed[HALF:]
    return jnp.concatenate([top * cos - bottom * sin, bottom * cos + top * sin], axis=0)


def heads_kernel(
    most_ref, w_ref, last_ref, qg_ref, kg_ref, cos_ref, sin_ref, q_ref, kv_ref, raw_ref
):
    cos, sin = cos_ref[...], sin_ref[...]
    raw_ref[...] = most_ref[...] + jnp.dot(
        w_ref[...], last_ref[...], preferred_element_type=f32
    )
    for h in range(2):
        rows = slice(h * HD, (h + 1) * HD)
        q_ref[rows, :] = rotate_norm(raw_ref[rows, :], qg_ref[...], cos, sin).astype(bf16)
    kv_ref[0:HD, :] = rotate_norm(raw_ref[2 * HD : 3 * HD, :], kg_ref[...], cos, sin).astype(bf16)
    kv_ref[HD : 2 * HD, :] = raw_ref[3 * HD : 4 * HD, :].astype(bf16)


def attend_kernel(
    ctx_ref, q_ref, raw_ref, own_ref, m1_ref, m2_ref, go_ref, qg_ref, cos_ref, sin_ref,
    dq_ref, d_own_ref, d_m1_ref, d_m2_ref, e_s, dp_s, dk_s, dv_s,
):
    ctx = ctx_ref[0]
    toks = q_ref.shape[1]
    sub = toks // 2
    cos, sin = cos_ref[...], sin_ref[...]
    blocks = (m2_ref, m1_ref, own_ref)

    def reach(b, i):
        first = 1 if b == 2 and i == 1 else 0
        last = 0 if b == 0 and i == 0 else 1
        return slice(first * sub, (last + 1) * sub), range(first, last + 1)

    for h in range(2):
        rows = slice(h * HD, (h + 1) * HD)
        q_t = q_ref[rows, :]
        q = q_t.T
        go = go_ref[:, rows]
        go_t = go.T
        totals, weights = ([jnp.zeros((1, sub), f32)] * 2 for _ in range(2))
        dqs = [jnp.zeros((HD, sub), f32)] * 2
        for b in range(3):
            k = blocks[b][0:HD, :].T
            v = blocks[b][HD : 2 * HD, :].T
            for i in range(2):
                at = slice(b * toks + i * sub, b * toks + (i + 1) * sub)
                own = slice(i * sub, (i + 1) * sub)
                cols, spans = reach(b, i)
                width = cols.stop - cols.start
                s = jnp.dot(k[own], q_t[:, cols], preferred_element_type=f32) * query_scale
                dp = jnp.dot(v[own], go_t[:, cols], preferred_element_type=f32).astype(bf16)
                key = lax.broadcasted_iota(jnp.int32, (sub, width), 0) + i * sub
                query = lax.broadcasted_iota(jnp.int32, (sub, width), 1) + cols.start
                if b == 0:
                    inside = (key > query) & (ctx >= 2)
                elif b == 1:
                    inside = (key >= 0) & (ctx >= 1)
                else:
                    inside = key <= query
                e = jnp.where(inside, jnp.exp(s), 0.0)
                e_s[at, cols] = e
                dp_s[at, cols] = dp
                part = jnp.sum(e, axis=0, keepdims=True)
                share = jnp.sum(e * dp.astype(f32), axis=0, keepdims=True)
                for n, j in enumerate(spans):
                    here = slice(n * sub, (n + 1) * sub)
                    totals[j] = totals[j] + part[:, here]
                    weights[j] = weights[j] + share[:, here]
        inv = 1.0 / jnp.concatenate(totals, axis=1)
        weighted = jnp.concatenate(weights, axis=1) * inv
        for b in range(3):
            for i in range(2):
                at = slice(b * toks + i * sub, b * toks + (i + 1) * sub)
                own = slice(i * sub, (i + 1) * sub)
                cols, spans = reach(b, i)
                p = e_s[at, cols] * inv[:, cols]
                ds = p * (dp_s[at, cols].astype(f32) - weighted[:, cols]) * query_scale
                ds = ds.astype(bf16)
                dv = jnp.dot(p.astype(bf16), go[cols], preferred_element_type=f32)
                dk = jnp.dot(ds, q[cols], preferred_element_type=f32)
                more = jnp.dot(blocks[b][0:HD, own], ds, preferred_element_type=f32)
                for n, j in enumerate(spans):
                    dqs[j] = dqs[j] + more[:, n * sub : (n + 1) * sub]
                if h == 0:
                    dk_s[at, :] = dk
                    dv_s[at, :] = dv
                else:
                    out = (d_m2_ref, d_m1_ref, d_own_ref)[b]
                    out[0, own, :] = (dk_s[at, :] + dk).astype(out.dtype)
                    out[1, own, :] = (dv_s[at, :] + dv).astype(out.dtype)
        dq_t = jnp.concatenate(dqs, axis=1)
        dq_low = dq_t.astype(bf16).astype(f32)
        dq_ref[rows, :] = unrotate_norm(dq_low, raw_ref[rows, :], qg_ref[...], cos, sin).astype(bf16)


def finish_kernel(dq_ref, own_ref, r1_ref, r2_ref, raw_ref, kg_ref, cos_ref, sin_ref, out_ref):
    def total(i):
        t = own_ref[i] + r1_ref[i].astype(f32) + r2_ref[i].astype(f32)
        return t.T.astype(bf16).astype(f32)

    out_ref[0 : 2 * HD, :] = dq_ref[...]
    out_ref[2 * HD : 3 * HD, :] = unrotate_norm(
        total(0), raw_ref[2 * HD : 3 * HD, :], kg_ref[...], cos_ref[...], sin_ref[...]
    ).astype(bf16)
    out_ref[3 * HD : 4 * HD, :] = total(1).astype(bf16)


def shards(hidden_in, w_query, w_key, w_value, q_gain, k_gain, grad_out):
    toks, feats = hidden_in.shape
    sds = jax.ShapeDtypeStruct
    ctx = lax.axis_index("ctx")
    tp = lax.axis_index("tp")
    core, j = ctx % NC, ctx // NC
    xh, y = tp // NY, tp % NY
    n_tp = NXH * NY
    blk = feats // 4

    def owner(rel):
        return ((xh + rel[0]) % NXH) * NY + (y + rel[1]) % NY

    positions = ctx * toks + lax.iota(jnp.int32, toks)
    freqs = jnp.exp(-math.log(rope_base) * (2.0 * jnp.arange(HALF, dtype=f32) / HD))
    angles = freqs[:, None] * positions.astype(f32)[None, :]
    cos, sin = jnp.cos(angles), jnp.sin(angles)
    qg, kg = q_gain[:, None], k_gain[:, None]

    w_cat = jnp.concatenate([w_query, w_key, w_value], axis=1)
    w_own = w_cat.reshape(n_tp, feats, w_cat.shape[1])

    table = jnp.stack([core, *[owner(rel) for rel in RELS + SENT]]).astype(jnp.int32)
    w_last = lax.dynamic_index_in_dim(w_own, owner(RELS[7]), 0, keepdims=False).T

    def project(total, parts, rels):
        for xs, rel in zip(parts, rels):
            ws = lax.dynamic_index_in_dim(w_own, owner(rel), 0, keepdims=False)
            term = lax.dot_general(ws, xs, (((0,), (0,)), ((), ())), preferred_element_type=f32)
            total = term if total is None else total + term
        return total

    begun = []

    def for_both(parts):
        x = jnp.stack(parts).reshape(len(parts), 2, NC, blk, toks)
        return x, lax.dynamic_index_in_dim(x, 1 - core, 2, keepdims=False)

    def beside(parts):
        begun.append(project(None, parts, RELS[:4]))
        begun.append(for_both(parts))
        return begun[0], *begun[1], cos, sin, w_last, table

    x_parts = gather_tp(hidden_in.T, beside)
    most = project(begun[0], x_parts[4:7], RELS[4:7])
    xb, ob = for_both(x_parts[4:7])
    last, most, xb, ob = lax.optimization_barrier((x_parts[7], most, xb, ob))

    low = sds((2 * HD, toks), bf16)
    q_t, kv_t, raw = call(heads_kernel, (low, low, sds(most.shape, f32)), 2.5)(
        most, w_last, last, qg, kg, cos, sin
    )
    rings = [[(a * NZ + z) * NC + c for z in range(NZ)] for a in range(NXL) for c in range(NC)]
    xl = j // NZ

    def x_specs(at):
        return [
            pl.BlockSpec((1, 2, 1, blk, toks), lambda i, t: (at(i), 0, t[0], 0, 0)),
            pl.BlockSpec((1, 2, blk, toks), lambda i, t: (at(i), 0, 0, 0)),
        ]

    def pair_spec(first):
        return pl.BlockSpec(
            (1, 2, 1, blk, 2 * toks),
            lambda i, t: (t[first + i] % NY, 0, t[first + i] // NY, 0, 0),
        )

    pair_shape = sds((NY, 2, NXH, blk, 2 * toks), bf16)

    def along_z(g):
        return lax.psum_scatter(
            g, "ctx", scatter_dimension=0, tiled=True, axis_index_groups=rings
        )[0]

    def across_x(g):
        g = g.reshape(NXL, blk, -1)
        keep = lax.dynamic_index_in_dim(g, xl, 0, keepdims=False)
        send = lax.dynamic_index_in_dim(g, 1 - xl, 0, keepdims=False)
        outs = [sds((blk, w), f32) for w in (2 * HD, HD, HD)]
        return call(add_pair, outs, 0.7)(keep, xlo_swap(send))

    kv1 = from_behind(kv_t, 1)
    kv2 = from_behind(kv_t, 2)
    xa, oa = begun[1]
    joined = with_table(
        join_first,
        4.0,
        (4,),
        tie((table,), kv_t)[0],
        x_specs(lambda i: i),
        (xa, core_swap(oa)),
        pair_shape,
        pair_spec(1),
    )
    kv2, joined = lax.optimization_barrier((kv2, joined))
    xc, oc = for_both(tie((last,), kv_t))
    pair = sds((2, toks, HD), bf16)
    dq_raw, d_own, d1, d2 = call(
        attend_kernel,
        (sds((2 * HD, toks), bf16), sds((2, toks, HD), f32), pair, pair),
        5.5,
        (
            pltpu.VMEM((3 * toks, toks), f32),
            pltpu.VMEM((3 * toks, toks), bf16),
            pltpu.VMEM((3 * toks, HD), f32),
            pltpu.VMEM((3 * toks, HD), f32),
        ),
        smem_first=True,
    )(ctx[None], q_t, raw, kv_t, kv1, kv2, grad_out, qg, cos, sin)
    r1 = from_behind(d1, -1)
    r2 = from_behind(d2, -2)
    x_pair = with_table(
        join_rest,
        4.0,
        (4,),
        tie((table,), dq_raw)[0],
        [
            *x_specs(lambda i: jnp.minimum(i, 2)),
            *x_specs(lambda i: 0),
            pl.BlockSpec(memory_space=pl.ANY),
        ],
        (xb, core_swap(ob), xc, core_swap(oc), joined),
        pair_shape,
        pair_spec(5),
        alias={5: 0},
    ).reshape(NZ, NXL * blk, 2 * toks)
    r1, r2, x_pair = lax.optimization_barrier((r1, r2, x_pair))
    d_all = call(finish_kernel, sds((4 * HD, toks), bf16), 1.3)(
        dq_raw, d_own, r1, r2, raw, kg, cos, sin
    )
    d_other = core_swap(d_all)

    def beside_tail(after):
        here, there, _ = lax.optimization_barrier((d_all, d_other, after))
        d_pair = jnp.concatenate([here, there], axis=1)
        g = lax.dot_general(x_pair, d_pair, (((2,), (1,)), ((), ())), preferred_element_type=f32)
        return g.astype(bf16)

    grad_input, g = scatter_tp(w_own, d_all, table, beside_tail)
    grad_input = grad_input.T
    grad_w = across_x(along_z(g))
    return (grad_input, *grad_w)


def solution(mesh):
    placed = (P("ctx", "tp"), P(None, "tp"), P(None, "tp"), P(None, "tp"), P(), P(), P("ctx", "tp"))
    return jax.shard_map(
        shards,
        mesh=mesh,
        in_specs=placed,
        out_specs=(P("ctx", "tp"), P("ctx", "tp"), P("ctx", "tp"), P("ctx", "tp")),
        check_vma=False,
    )
```

```python
import functools
import math

import jax
import jax.numpy as jnp
from jax import lax
from jax.experimental import pallas as pl
from jax.experimental.pallas import tpu as pltpu
from jax.sharding import PartitionSpec as P

WINDOW = 1024
HD = 128
HALF = 64
NY, NXH = 4, 2
NXL, NZ, NC = 2, 8, 2

query_scale = 1.0 / math.sqrt(168.0)
rope_base = 10000.0
norm_eps = 1e-06
f32 = jnp.float32
bf16 = jnp.bfloat16
VMEM = pl.BlockSpec(memory_space=pltpu.VMEM)


def tp_perm(dx, dy):
    return [
        (x * NY + y, ((x + dx) % NXH) * NY + (y + dy) % NY)
        for x in range(NXH)
        for y in range(NY)
    ]


def y_step(v, d):
    return lax.ppermute(v, "tp", tp_perm(0, d))


def x_swap(v):
    return lax.ppermute(v, "tp", tp_perm(1, 0))


def core_swap(v):
    return lax.ppermute(v, "ctx", [(i, i ^ 1) for i in range(NXL * NZ * NC)])


def xlo_swap(v):
    n = NXL * NZ * NC
    return lax.ppermute(v, "ctx", [(i, (i + n // 2) % n) for i in range(n)])


def from_behind(block, distance):
    n = NXL * NZ * NC
    route = [(i - distance, i) for i in range(n) if 0 <= i - distance < n]
    return lax.ppermute(block, "ctx", route)


def tie(values, *after):
    return lax.optimization_barrier((*values, *after))[: len(values)]


RELS = [(0, 0), (0, 3), (0, 1), (1, 0), (0, 2), (1, 3), (1, 1), (1, 2)]
SENT = [(1, 2), (0, 2), (1, 3), (1, 1), (1, 0), (0, 3), (0, 1), (0, 0)]


def gather_tp(own, beside_second):
    half = own.shape[0] // 2
    below = y_step(own, 1)
    above = y_step(own, -1)
    across = x_swap(own)
    second = (
        jnp.concatenate([below[:half], across[half:]]),
        jnp.concatenate([across[:half], above[half:]]),
        jnp.concatenate([below[:half], above[half:]]),
    )
    up = y_step(second[0], 1)
    down = y_step(second[1], -1)
    side = x_swap(second[2])
    far = jnp.concatenate([up[:half], down[half:]])
    x_below = jnp.concatenate([side[:half], up[half:]])
    x_above = jnp.concatenate([down[:half], side[half:]])
    third = tie((side[:half], side[half:]), *beside_second([own, below, above, across]))
    far_up = y_step(third[0], 1)
    far_down = y_step(third[1], -1)
    x_far = jnp.concatenate([far_up, far_down])
    return [own, below, above, across, far, x_below, x_above, x_far]


def cost(us):
    return pl.CostEstimate(flops=0, bytes_accessed=int(us * 3.4e6), transcendentals=0)


def call(kernel, outs, us, scratch=(), smem_first=False, mib=40):
    def run(*args):
        in_specs = [VMEM] * len(args)
        if smem_first:
            in_specs[0] = pl.BlockSpec(memory_space=pltpu.SMEM)
        return pl.pallas_call(
            kernel,
            out_shape=outs,
            in_specs=in_specs,
            out_specs=jax.tree.map(lambda _: VMEM, outs),
            scratch_shapes=list(scratch),
            compiler_params=pltpu.CompilerParams(vmem_limit_bytes=mib * 2**20),
            cost_estimate=cost(us),
        )(*args)

    return run


def halves(ref):
    half = ref.shape[-2] // 2
    return slice(0, half), slice(half, 2 * half)


def add_pair(g_ref, got_ref, q_ref, k_ref, v_ref):
    total = g_ref[0].astype(f32) + got_ref[...].astype(f32)
    q_ref[...] = total[:, : 2 * HD]
    k_ref[...] = total[:, 2 * HD : 3 * HD]
    v_ref[...] = total[:, 3 * HD :]


def first_terms(own_ref, w_ref, d_ref, top_ref, bottom_ref):
    t = jnp.dot(w_ref[0], d_ref[...], preferred_element_type=f32).astype(bf16)
    lo, hi = halves(w_ref)
    top_ref[...] = t[lo]
    bottom_ref[...] = t[hi]


def second_terms(own_ref, w_ref, d_ref, side_ref, down_ref, up_ref):
    lo, hi = halves(w_ref)
    i = pl.program_id(0)
    t = jnp.dot(w_ref[0], d_ref[...], preferred_element_type=f32).astype(bf16)

    @pl.when(i == 0)
    def _():
        down_ref[lo, :] = t[lo]
        up_ref[hi, :] = t[hi]

    @pl.when(i == 1)
    def _():
        side_ref[lo, :] = t[lo]
        down_ref[hi, :] = t[hi]

    @pl.when(i == 2)
    def _():
        up_ref[lo, :] = t[lo]
        side_ref[hi, :] = t[hi]


def third_terms(own_ref, w_ref, d_ref, across_ref, below_ref, above_ref, mine_ref):
    i = pl.program_id(0)
    t = jnp.dot(w_ref[0], d_ref[...], preferred_element_type=f32)
    for n, ref in enumerate((across_ref, below_ref, above_ref, mine_ref)):

        @pl.when(i == n)
        def _(ref=ref):
            ref[...] = t.astype(ref.dtype)


def add_side(side_ref, top_ref, bottom_ref, out_ref):
    lo, hi = halves(side_ref)
    out_ref[lo, :] = (side_ref[lo, :].astype(f32) + top_ref[...].astype(f32)).astype(bf16)
    out_ref[hi, :] = (side_ref[hi, :].astype(f32) + bottom_ref[...].astype(f32)).astype(bf16)


def add_across(term_ref, down_ref, up_ref, out_ref):
    lo, hi = halves(term_ref)
    out_ref[lo, :] = (term_ref[lo, :].astype(f32) + up_ref[lo, :].astype(f32)).astype(bf16)
    out_ref[hi, :] = (term_ref[hi, :].astype(f32) + down_ref[hi, :].astype(f32)).astype(bf16)


def add_near(below_ref, above_ref, side_ref, down_ref, up_ref, out_b_ref, out_a_ref):
    lo, hi = halves(below_ref)
    more_b = side_ref[lo, :].astype(f32) + down_ref[lo, :].astype(f32)
    more_a = side_ref[hi, :].astype(f32) + up_ref[hi, :].astype(f32)
    out_b_ref[lo, :] = (below_ref[lo, :].astype(f32) + more_b).astype(bf16)
    out_b_ref[hi, :] = below_ref[hi, :]
    out_a_ref[lo, :] = above_ref[lo, :]
    out_a_ref[hi, :] = (above_ref[hi, :].astype(f32) + more_a).astype(bf16)


def add_last(mine_ref, a_ref, b_ref, c_ref, out_ref):
    got = a_ref[...].astype(f32) + b_ref[...].astype(f32) + c_ref[...].astype(f32)
    out_ref[...] = (mine_ref[...].astype(f32) + got).astype(bf16)


def with_table(kernel, us, grid, table, specs, args, outs, out_specs, scratch=(), alias={}):
    return pl.pallas_call(
        kernel,
        out_shape=outs,
        grid_spec=pltpu.PrefetchScalarGridSpec(
            num_scalar_prefetch=1,
            grid=grid,
            in_specs=specs,
            out_specs=out_specs,
            scratch_shapes=list(scratch),
        ),
        compiler_params=pltpu.CompilerParams(vmem_limit_bytes=56 * 2**20),
        cost_estimate=cost(us),
        input_output_aliases=alias,
    )(table, *args)


def scatter_tp(w_own, d_all, table, beside):
    _, feats, cols = w_own.shape
    toks = d_all.shape[1]
    sds = jax.ShapeDtypeStruct
    full, part = sds((feats, toks), bf16), sds((feats // 2, toks), bf16)

    def terms(kernel, us, first, count, outs, after=None):
        whole = lambda v: pl.BlockSpec(v.shape, lambda i, t: (0,) * len(v.shape))
        at = 1 + len(RELS) + first
        return with_table(
            kernel,
            us,
            (count,),
            table if after is None else tie((table,), after)[0],
            [
                pl.BlockSpec((1, feats, cols), lambda i, t: (t[at + i], 0, 0)),
                whole(d_all),
            ],
            (w_own, d_all),
            outs,
            [whole(o) for o in outs],
        )

    top, bottom = terms(first_terms, 2.0, 0, 1, [part, part])
    extra = beside(top)
    top, bottom = y_step(top, -1), y_step(bottom, 1)
    side, down, up = terms(second_terms, 4.5, 1, 3, [full] * 3, extra)
    down, up = y_step(down, -1), y_step(up, 1)
    side = x_swap(call(add_side, full, 0.8)(side, top, bottom))
    across, below, above, mine = terms(third_terms, 6.0, 4, 4, [full] * 4)
    down, up, across, below, above = lax.optimization_barrier((down, up, across, below, above))
    across = x_swap(call(add_across, full, 0.8)(across, down, up))
    below, above = call(add_near, (full, full), 1.2)(below, above, side, down, up)
    below, above = y_step(below, -1), y_step(above, 1)
    return call(add_last, full, 1.5)(mine, across, below, above), extra


def join_first(table_ref, x_ref, o_ref, out_ref):
    toks = o_ref.shape[3]
    for i in range(2):
        out_ref[0, i, 0, :, :toks] = x_ref[0, i, 0]
        out_ref[0, i, 0, :, toks:] = o_ref[0, i]


def join_rest(table_ref, xb_ref, ob_ref, xc_ref, oc_ref, begun_ref, out_ref):
    step = pl.program_id(0)
    pl.when(step < 3)(lambda: join_first(table_ref, xb_ref, ob_ref, out_ref))
    pl.when(step == 3)(lambda: join_first(table_ref, xc_ref, oc_ref, out_ref))


def unrotate_norm(grad, raw, gain, cos, sin):
    top, bottom = grad[:HALF], grad[HALF:]
    d_normed = jnp.concatenate([top * cos + bottom * sin, bottom * cos - top * sin], axis=0)
    inv = lax.rsqrt(jnp.mean(raw * raw, axis=0, keepdims=True) + norm_eps)
    scaled = d_normed * gain
    along = jnp.mean(raw * scaled, axis=0, keepdims=True)
    return inv * scaled - raw * (inv * inv * inv * along)


def rotate_norm(raw, gain, cos, sin):
    inv = lax.rsqrt(jnp.mean(raw * raw, axis=0, keepdims=True) + norm_eps)
    normed = raw * inv * gain
    top, bottom = normed[:HALF], normed[HALF:]
    return jnp.concatenate([top * cos - bottom * sin, bottom * cos + top * sin], axis=0)


def heads_kernel(
    most_ref, w_ref, last_ref, qg_ref, kg_ref, cos_ref, sin_ref, q_ref, kv_ref, raw_ref
):
    cos, sin = cos_ref[...], sin_ref[...]
    raw_ref[...] = most_ref[...] + jnp.dot(
        w_ref[...], last_ref[...], preferred_element_type=f32
    )
    for h in range(2):
        rows = slice(h * HD, (h + 1) * HD)
        q_ref[rows, :] = rotate_norm(raw_ref[rows, :], qg_ref[...], cos, sin).astype(bf16)
    kv_ref[0:HD, :] = rotate_norm(raw_ref[2 * HD : 3 * HD, :], kg_ref[...], cos, sin).astype(bf16)
    kv_ref[HD : 2 * HD, :] = raw_ref[3 * HD : 4 * HD, :].astype(bf16)


def attend_kernel(
    ctx_ref, q_ref, raw_ref, own_ref, m1_ref, m2_ref, go_ref, qg_ref, cos_ref, sin_ref,
    dq_ref, d_own_ref, d_m1_ref, d_m2_ref, e_s, dp_s, dk_s, dv_s,
):
    ctx = ctx_ref[0]
    toks = q_ref.shape[1]
    sub = toks // 2
    cos, sin = cos_ref[...], sin_ref[...]
    blocks = (m2_ref, m1_ref, own_ref)

    def reach(b, i):
        first = 1 if b == 2 and i == 1 else 0
        last = 0 if b == 0 and i == 0 else 1
        return slice(first * sub, (last + 1) * sub), range(first, last + 1)

    for h in range(2):
        rows = slice(h * HD, (h + 1) * HD)
        q_t = q_ref[rows, :]
        q = q_t.T
        go = go_ref[:, rows]
        go_t = go.T
        totals, weights = ([jnp.zeros((1, sub), f32)] * 2 for _ in range(2))
        dqs = [jnp.zeros((HD, sub), f32)] * 2
        for b in range(3):
            k = blocks[b][0:HD, :].T
            v = blocks[b][HD : 2 * HD, :].T
            for i in range(2):
                at = slice(b * toks + i * sub, b * toks + (i + 1) * sub)
                own = slice(i * sub, (i + 1) * sub)
                cols, spans = reach(b, i)
                width = cols.stop - cols.start
                s = jnp.dot(k[own], q_t[:, cols], preferred_element_type=f32) * query_scale
                dp = jnp.dot(v[own], go_t[:, cols], preferred_element_type=f32).astype(bf16)
                key = lax.broadcasted_iota(jnp.int32, (sub, width), 0) + i * sub
                query = lax.broadcasted_iota(jnp.int32, (sub, width), 1) + cols.start
                if b == 0:
                    inside = (key > query) & (ctx >= 2)
                elif b == 1:
                    inside = (key >= 0) & (ctx >= 1)
                else:
                    inside = key <= query
                e = jnp.where(inside, jnp.exp(s), 0.0)
                e_s[at, cols] = e
                dp_s[at, cols] = dp
                part = jnp.sum(e, axis=0, keepdims=True)
                share = jnp.sum(e * dp.astype(f32), axis=0, keepdims=True)
                for n, j in enumerate(spans):
                    here = slice(n * sub, (n + 1) * sub)
                    totals[j] = totals[j] + part[:, here]
                    weights[j] = weights[j] + share[:, here]
        inv = 1.0 / jnp.concatenate(totals, axis=1)
        weighted = jnp.concatenate(weights, axis=1) * inv
        for b in range(3):
            for i in range(2):
                at = slice(b * toks + i * sub, b * toks + (i + 1) * sub)
                own = slice(i * sub, (i + 1) * sub)
                cols, spans = reach(b, i)
                p = e_s[at, cols] * inv[:, cols]
                ds = p * (dp_s[at, cols].astype(f32) - weighted[:, cols]) * query_scale
                ds = ds.astype(bf16)
                dv = jnp.dot(p.astype(bf16), go[cols], preferred_element_type=f32)
                dk = jnp.dot(ds, q[cols], preferred_element_type=f32)
                more = jnp.dot(blocks[b][0:HD, own], ds, preferred_element_type=f32)
                for n, j in enumerate(spans):
                    dqs[j] = dqs[j] + more[:, n * sub : (n + 1) * sub]
                if h == 0:
                    dk_s[at, :] = dk
                    dv_s[at, :] = dv
                else:
                    out = (d_m2_ref, d_m1_ref, d_own_ref)[b]
                    out[0, own, :] = (dk_s[at, :] + dk).astype(out.dtype)
                    out[1, own, :] = (dv_s[at, :] + dv).astype(out.dtype)
        dq_t = jnp.concatenate(dqs, axis=1)
        dq_low = dq_t.astype(bf16).astype(f32)
        dq_ref[rows, :] = unrotate_norm(dq_low, raw_ref[rows, :], qg_ref[...], cos, sin).astype(bf16)


def finish_kernel(dq_ref, own_ref, r1_ref, r2_ref, raw_ref, kg_ref, cos_ref, sin_ref, out_ref):
    def total(i):
        t = own_ref[i] + r1_ref[i].astype(f32) + r2_ref[i].astype(f32)
        return t.T.astype(bf16).astype(f32)

    out_ref[0 : 2 * HD, :] = dq_ref[...]
    out_ref[2 * HD : 3 * HD, :] = unrotate_norm(
        total(0), raw_ref[2 * HD : 3 * HD, :], kg_ref[...], cos_ref[...], sin_ref[...]
    ).astype(bf16)
    out_ref[3 * HD : 4 * HD, :] = total(1).astype(bf16)


def shards(hidden_in, w_query, w_key, w_value, q_gain, k_gain, grad_out):
    toks, feats = hidden_in.shape
    sds = jax.ShapeDtypeStruct
    ctx = lax.axis_index("ctx")
    tp = lax.axis_index("tp")
    core, j = ctx % NC, ctx // NC
    xh, y = tp // NY, tp % NY
    n_tp = NXH * NY
    blk = feats // 4

    def owner(rel):
        return ((xh + rel[0]) % NXH) * NY + (y + rel[1]) % NY

    positions = ctx * toks + lax.iota(jnp.int32, toks)
    freqs = jnp.exp(-math.log(rope_base) * (2.0 * jnp.arange(HALF, dtype=f32) / HD))
    angles = freqs[:, None] * positions.astype(f32)[None, :]
    cos, sin = jnp.cos(angles), jnp.sin(angles)
    qg, kg = q_gain[:, None], k_gain[:, None]

    w_cat = jnp.concatenate([w_query, w_key, w_value], axis=1)
    w_own = w_cat.reshape(n_tp, feats, w_cat.shape[1])

    table = jnp.stack([core, *[owner(rel) for rel in RELS + SENT], j // NZ]).astype(jnp.int32)
    w_last = lax.dynamic_index_in_dim(w_own, owner(RELS[7]), 0, keepdims=False).T

    def project(total, parts, rels):
        for xs, rel in zip(parts, rels):
            ws = lax.dynamic_index_in_dim(w_own, owner(rel), 0, keepdims=False)
            term = lax.dot_general(ws, xs, (((0,), (0,)), ((), ())), preferred_element_type=f32)
            total = term if total is None else total + term
        return total

    begun = []

    def for_both(parts):
        x = jnp.stack(parts).reshape(len(parts), 2, NC, blk, toks)
        return x, lax.dynamic_index_in_dim(x, 1 - core, 2, keepdims=False)

    def beside(parts):
        begun.append(project(None, parts, RELS[:4]))
        begun.append(for_both(parts))
        return begun[0], *begun[1], cos, sin, w_last, table

    x_parts = gather_tp(hidden_in.T, beside)
    most = project(begun[0], x_parts[4:7], RELS[4:7])
    xb, ob = for_both(x_parts[4:7])
    last, most, xb, ob = lax.optimization_barrier((x_parts[7], most, xb, ob))

    low = sds((2 * HD, toks), bf16)
    q_t, kv_t, raw = call(heads_kernel, (low, low, sds(most.shape, f32)), 2.5)(
        most, w_last, last, qg, kg, cos, sin
    )
    rings = [[(a * NZ + z) * NC + c for z in range(NZ)] for a in range(NXL) for c in range(NC)]

    def x_specs(at):
        return [
            pl.BlockSpec((1, 2, 1, blk, toks), lambda i, t: (at(i), 0, t[0], 0, 0)),
            pl.BlockSpec((1, 2, blk, toks), lambda i, t: (at(i), 0, 0, 0)),
        ]

    def pair_spec(first):
        half = 1 + len(RELS + SENT)
        return pl.BlockSpec(
            (1, 2, 1, blk, 2 * toks),
            lambda i, t: (t[first + i] % NY, 0, (t[first + i] // NY + t[half]) % NXL, 0, 0),
        )

    pair_shape = sds((NY, 2, NXH, blk, 2 * toks), bf16)

    def along_z(g):
        return lax.psum_scatter(
            g, "ctx", scatter_dimension=0, tiled=True, axis_index_groups=rings
        )[0]

    def across_x(g):
        g = g.reshape(NXL, blk, -1)
        outs = [sds((blk, w), f32) for w in (2 * HD, HD, HD)]
        return call(add_pair, outs, 0.7)(g, xlo_swap(g[1]))

    kv1 = from_behind(kv_t, 1)
    kv2 = from_behind(kv_t, 2)
    xa, oa = begun[1]
    joined = with_table(
        join_first,
        4.0,
        (4,),
        tie((table,), kv_t)[0],
        x_specs(lambda i: i),
        (xa, core_swap(oa)),
        pair_shape,
        pair_spec(1),
    )
    kv2, joined = lax.optimization_barrier((kv2, joined))
    xc, oc = for_both(tie((last,), kv_t))
    pair = sds((2, toks, HD), bf16)
    dq_raw, d_own, d1, d2 = call(
        attend_kernel,
        (sds((2 * HD, toks), bf16), sds((2, toks, HD), f32), pair, pair),
        5.5,
        (
            pltpu.VMEM((3 * toks, toks), f32),
            pltpu.VMEM((3 * toks, toks), bf16),
            pltpu.VMEM((3 * toks, HD), f32),
            pltpu.VMEM((3 * toks, HD), f32),
        ),
        smem_first=True,
    )(ctx[None], q_t, raw, kv_t, kv1, kv2, grad_out, qg, cos, sin)
    r1 = from_behind(d1, -1)
    r2 = from_behind(d2, -2)
    x_pair = with_table(
        join_rest,
        4.0,
        (4,),
        tie((table,), dq_raw)[0],
        [
            *x_specs(lambda i: jnp.minimum(i, 2)),
            *x_specs(lambda i: 0),
            pl.BlockSpec(memory_space=pl.ANY),
        ],
        (xb, core_swap(ob), xc, core_swap(oc), joined),
        pair_shape,
        pair_spec(5),
        alias={5: 0},
    ).reshape(NZ, NXL * blk, 2 * toks)
    r1, r2, x_pair = lax.optimization_barrier((r1, r2, x_pair))
    d_all = call(finish_kernel, sds((4 * HD, toks), bf16), 1.3)(
        dq_raw, d_own, r1, r2, raw, kg, cos, sin
    )
    d_other = core_swap(d_all)

    def beside_tail(after):
        here, there, _ = lax.optimization_barrier((d_all, d_other, after))
        d_pair = jnp.concatenate([here, there], axis=1)
        g = lax.dot_general(x_pair, d_pair, (((2,), (1,)), ((), ())), preferred_element_type=f32)
        return g.astype(bf16)

    grad_input, g = scatter_tp(w_own, d_all, table, beside_tail)
    grad_input = grad_input.T
    grad_w = across_x(along_z(g))
    return (grad_input, *grad_w)


def solution(mesh):
    placed = (P("ctx", "tp"), P(None, "tp"), P(None, "tp"), P(None, "tp"), P(), P(), P("ctx", "tp"))
    return jax.shard_map(
        shards,
        mesh=mesh,
        in_specs=placed,
        out_specs=(P("ctx", "tp"), P("ctx", "tp"), P("ctx", "tp"), P("ctx", "tp")),
        check_vma=False,
    )
```

```python
import functools
import math

import jax
import jax.numpy as jnp
from jax import lax
from jax.experimental import pallas as pl
from jax.experimental.pallas import tpu as pltpu
from jax.sharding import PartitionSpec as P

WINDOW = 1024
HD = 128
HALF = 64
NY, NXH = 4, 2
NXL, NZ, NC = 2, 8, 2

query_scale = 1.0 / math.sqrt(168.0)
rope_base = 10000.0
norm_eps = 1e-06
f32 = jnp.float32
bf16 = jnp.bfloat16
VMEM = pl.BlockSpec(memory_space=pltpu.VMEM)


def tp_perm(dx, dy):
    return [
        (x * NY + y, ((x + dx) % NXH) * NY + (y + dy) % NY)
        for x in range(NXH)
        for y in range(NY)
    ]


def y_step(v, d):
    return lax.ppermute(v, "tp", tp_perm(0, d))


def x_swap(v):
    return lax.ppermute(v, "tp", tp_perm(1, 0))


def core_swap(v):
    return lax.ppermute(v, "ctx", [(i, i ^ 1) for i in range(NXL * NZ * NC)])


def xlo_swap(v):
    n = NXL * NZ * NC
    return lax.ppermute(v, "ctx", [(i, (i + n // 2) % n) for i in range(n)])


def from_behind(block, distance):
    n = NXL * NZ * NC
    route = [(i - distance, i) for i in range(n) if 0 <= i - distance < n]
    return lax.ppermute(block, "ctx", route)


def tie(values, *after):
    return lax.optimization_barrier((*values, *after))[: len(values)]


RELS = [(0, 0), (0, 3), (0, 1), (1, 0), (0, 2), (1, 3), (1, 1), (1, 2)]
SENT = [(1, 2), (0, 2), (1, 3), (1, 1), (1, 0), (0, 3), (0, 1), (0, 0)]


def gather_tp(own, beside_second):
    half = own.shape[0] // 2
    below = y_step(own, 1)
    above = y_step(own, -1)
    across = x_swap(own)
    second = (
        jnp.concatenate([below[:half], across[half:]]),
        jnp.concatenate([across[:half], above[half:]]),
        jnp.concatenate([below[:half], above[half:]]),
    )
    up = y_step(second[0], 1)
    down = y_step(second[1], -1)
    side = x_swap(second[2])
    far = jnp.concatenate([up[:half], down[half:]])
    x_below = jnp.concatenate([side[:half], up[half:]])
    x_above = jnp.concatenate([down[:half], side[half:]])
    third = tie((side[:half], side[half:]), *beside_second([own, below, above, across]))
    far_up = y_step(third[0], 1)
    far_down = y_step(third[1], -1)
    x_far = jnp.concatenate([far_up, far_down])
    return [own, below, above, across, far, x_below, x_above, x_far]


def cost(us):
    return pl.CostEstimate(flops=0, bytes_accessed=int(us * 3.4e6), transcendentals=0)


def call(kernel, outs, us, scratch=(), smem_first=False, mib=40):
    def run(*args):
        in_specs = [VMEM] * len(args)
        if smem_first:
            in_specs[0] = pl.BlockSpec(memory_space=pltpu.SMEM)
        return pl.pallas_call(
            kernel,
            out_shape=outs,
            in_specs=in_specs,
            out_specs=jax.tree.map(lambda _: VMEM, outs),
            scratch_shapes=list(scratch),
            compiler_params=pltpu.CompilerParams(vmem_limit_bytes=mib * 2**20),
            cost_estimate=cost(us),
        )(*args)

    return run


def halves(ref):
    half = ref.shape[-2] // 2
    return slice(0, half), slice(half, 2 * half)


def add_pair(g_ref, got_ref, q_ref, k_ref, v_ref):
    total = g_ref[0].astype(f32) + got_ref[...].astype(f32)
    q_ref[...] = total[:, : 2 * HD]
    k_ref[...] = total[:, 2 * HD : 3 * HD]
    v_ref[...] = total[:, 3 * HD :]


def first_terms(own_ref, w_ref, d_ref, top_ref, bottom_ref):
    t = jnp.dot(w_ref[0], d_ref[...], preferred_element_type=f32).astype(bf16)
    for n, ref in enumerate((top_ref, bottom_ref)):

        @pl.when(pl.program_id(0) == n)
        def _(ref=ref):
            ref[...] = t


def second_terms(own_ref, w_ref, d_ref, side_ref, down_ref, up_ref):
    lo, hi = halves(w_ref)
    i = pl.program_id(0)
    t = jnp.dot(w_ref[0], d_ref[...], preferred_element_type=f32).astype(bf16)

    @pl.when(i == 0)
    def _():
        down_ref[lo, :] = t[lo]
        up_ref[hi, :] = t[hi]

    @pl.when(i == 1)
    def _():
        side_ref[lo, :] = t[lo]
        down_ref[hi, :] = t[hi]

    @pl.when(i == 2)
    def _():
        up_ref[lo, :] = t[lo]
        side_ref[hi, :] = t[hi]


def third_terms(own_ref, w_ref, d_ref, across_ref, below_ref, above_ref, mine_ref):
    i = pl.program_id(0)
    t = jnp.dot(w_ref[0], d_ref[...], preferred_element_type=f32)
    for n, ref in enumerate((across_ref, below_ref, above_ref, mine_ref)):

        @pl.when(i == n)
        def _(ref=ref):
            ref[...] = t.astype(ref.dtype)


def add_side(side_ref, top_ref, bottom_ref, out_ref):
    lo, hi = halves(side_ref)
    out_ref[lo, :] = (side_ref[lo, :].astype(f32) + top_ref[...].astype(f32)).astype(bf16)
    out_ref[hi, :] = (side_ref[hi, :].astype(f32) + bottom_ref[...].astype(f32)).astype(bf16)


def add_across(term_ref, down_ref, up_ref, out_ref):
    lo, hi = halves(term_ref)
    out_ref[lo, :] = (term_ref[lo, :].astype(f32) + up_ref[lo, :].astype(f32)).astype(bf16)
    out_ref[hi, :] = (term_ref[hi, :].astype(f32) + down_ref[hi, :].astype(f32)).astype(bf16)


def add_near(below_ref, above_ref, side_ref, down_ref, up_ref, out_b_ref, out_a_ref):
    lo, hi = halves(below_ref)
    more_b = side_ref[lo, :].astype(f32) + down_ref[lo, :].astype(f32)
    more_a = side_ref[hi, :].astype(f32) + up_ref[hi, :].astype(f32)
    out_b_ref[lo, :] = (below_ref[lo, :].astype(f32) + more_b).astype(bf16)
    out_b_ref[hi, :] = below_ref[hi, :]
    out_a_ref[lo, :] = above_ref[lo, :]
    out_a_ref[hi, :] = (above_ref[hi, :].astype(f32) + more_a).astype(bf16)


def add_last(mine_ref, a_ref, b_ref, c_ref, out_ref):
    got = a_ref[...].astype(f32) + b_ref[...].astype(f32) + c_ref[...].astype(f32)
    out_ref[...] = (mine_ref[...].astype(f32) + got).astype(bf16)


def with_table(kernel, us, grid, table, specs, args, outs, out_specs, scratch=(), alias={}):
    return pl.pallas_call(
        kernel,
        out_shape=outs,
        grid_spec=pltpu.PrefetchScalarGridSpec(
            num_scalar_prefetch=1,
            grid=grid,
            in_specs=specs,
            out_specs=out_specs,
            scratch_shapes=list(scratch),
        ),
        compiler_params=pltpu.CompilerParams(vmem_limit_bytes=56 * 2**20),
        cost_estimate=cost(us),
        input_output_aliases=alias,
    )(table, *args)


def scatter_tp(w_own, d_all, table, beside):
    _, feats, cols = w_own.shape
    toks = d_all.shape[1]
    sds = jax.ShapeDtypeStruct
    full, part = sds((feats, toks), bf16), sds((feats // 2, toks), bf16)

    def terms(kernel, us, first, count, outs, after=None):
        whole = lambda v: pl.BlockSpec(v.shape, lambda i, t: (0,) * len(v.shape))
        at = 1 + len(RELS) + first
        return with_table(
            kernel,
            us,
            (count,),
            table if after is None else tie((table,), after)[0],
            [
                pl.BlockSpec((1, feats, cols), lambda i, t: (t[at + i], 0, 0)),
                whole(d_all),
            ],
            (w_own, d_all),
            outs,
            [whole(o) for o in outs],
        )

    whole = lambda v: pl.BlockSpec(v.shape, lambda i, t: (0,) * len(v.shape))
    to_far = 1 + len(RELS)
    top, bottom = with_table(
        first_terms,
        2.0,
        (2,),
        table,
        [
            pl.BlockSpec((1, feats // 2, cols), lambda i, t: (t[to_far], i, 0)),
            whole(d_all),
        ],
        (w_own, d_all),
        [part, part],
        [whole(part), whole(part)],
    )
    extra = beside(top)
    top, bottom = y_step(top, -1), y_step(bottom, 1)
    side, down, up = terms(second_terms, 4.5, 1, 3, [full] * 3, extra)
    down, up = y_step(down, -1), y_step(up, 1)
    side = x_swap(call(add_side, full, 0.8)(side, top, bottom))
    across, below, above, mine = terms(third_terms, 6.0, 4, 4, [full] * 4)
    down, up, across, below, above = lax.optimization_barrier((down, up, across, below, above))
    across = x_swap(call(add_across, full, 0.8)(across, down, up))
    below, above = call(add_near, (full, full), 1.2)(below, above, side, down, up)
    below, above = y_step(below, -1), y_step(above, 1)
    return call(add_last, full, 1.5)(mine, across, below, above), extra


def join_first(table_ref, x_ref, o_ref, out_ref):
    toks = o_ref.shape[3]
    for i in range(2):
        out_ref[0, i, 0, :, :toks] = x_ref[0, i, 0]
        out_ref[0, i, 0, :, toks:] = o_ref[0, i]


def join_rest(table_ref, xb_ref, ob_ref, xc_ref, oc_ref, begun_ref, out_ref):
    step = pl.program_id(0)
    pl.when(step < 3)(lambda: join_first(table_ref, xb_ref, ob_ref, out_ref))
    pl.when(step == 3)(lambda: join_first(table_ref, xc_ref, oc_ref, out_ref))


def unrotate_norm(grad, raw, gain, cos, sin):
    top, bottom = grad[:HALF], grad[HALF:]
    d_normed = jnp.concatenate([top * cos + bottom * sin, bottom * cos - top * sin], axis=0)
    inv = lax.rsqrt(jnp.mean(raw * raw, axis=0, keepdims=True) + norm_eps)
    scaled = d_normed * gain
    along = jnp.mean(raw * scaled, axis=0, keepdims=True)
    return inv * scaled - raw * (inv * inv * inv * along)


def rotate_norm(raw, gain, cos, sin):
    inv = lax.rsqrt(jnp.mean(raw * raw, axis=0, keepdims=True) + norm_eps)
    normed = raw * inv * gain
    top, bottom = normed[:HALF], normed[HALF:]
    return jnp.concatenate([top * cos - bottom * sin, bottom * cos + top * sin], axis=0)


def heads_kernel(
    most_ref, w_ref, last_ref, qg_ref, kg_ref, cos_ref, sin_ref, q_ref, kv_ref, raw_ref
):
    cos, sin = cos_ref[...], sin_ref[...]
    raw_ref[...] = most_ref[...] + jnp.dot(
        w_ref[...], last_ref[...], preferred_element_type=f32
    )
    for h in range(2):
        rows = slice(h * HD, (h + 1) * HD)
        q_ref[rows, :] = rotate_norm(raw_ref[rows, :], qg_ref[...], cos, sin).astype(bf16)
    kv_ref[0:HD, :] = rotate_norm(raw_ref[2 * HD : 3 * HD, :], kg_ref[...], cos, sin).astype(bf16)
    kv_ref[HD : 2 * HD, :] = raw_ref[3 * HD : 4 * HD, :].astype(bf16)


def attend_kernel(
    ctx_ref, q_ref, raw_ref, own_ref, m1_ref, m2_ref, go_ref, qg_ref, cos_ref, sin_ref,
    dq_ref, d_own_ref, d_m1_ref, d_m2_ref, e_s, dp_s, dk_s, dv_s,
):
    ctx = ctx_ref[0]
    toks = q_ref.shape[1]
    sub = toks // 2
    cos, sin = cos_ref[...], sin_ref[...]
    blocks = (m2_ref, m1_ref, own_ref)

    def reach(b, i):
        first = 1 if b == 2 and i == 1 else 0
        last = 0 if b == 0 and i == 0 else 1
        return slice(first * sub, (last + 1) * sub), range(first, last + 1)

    for h in range(2):
        rows = slice(h * HD, (h + 1) * HD)
        q_t = q_ref[rows, :]
        q = q_t.T
        go = go_ref[:, rows]
        go_t = go.T
        totals, weights = ([jnp.zeros((1, sub), f32)] * 2 for _ in range(2))
        dqs = [jnp.zeros((HD, sub), f32)] * 2
        for b in range(3):
            k = blocks[b][0:HD, :].T
            v = blocks[b][HD : 2 * HD, :].T
            for i in range(2):
                at = slice(b * toks + i * sub, b * toks + (i + 1) * sub)
                own = slice(i * sub, (i + 1) * sub)
                cols, spans = reach(b, i)
                width = cols.stop - cols.start
                s = jnp.dot(k[own], q_t[:, cols], preferred_element_type=f32) * query_scale
                dp = jnp.dot(v[own], go_t[:, cols], preferred_element_type=f32).astype(bf16)
                key = lax.broadcasted_iota(jnp.int32, (sub, width), 0) + i * sub
                query = lax.broadcasted_iota(jnp.int32, (sub, width), 1) + cols.start
                if b == 0:
                    inside = (key > query) & (ctx >= 2)
                elif b == 1:
                    inside = (key >= 0) & (ctx >= 1)
                else:
                    inside = key <= query
                e = jnp.where(inside, jnp.exp(s), 0.0)
                e_s[at, cols] = e
                dp_s[at, cols] = dp
                part = jnp.sum(e, axis=0, keepdims=True)
                share = jnp.sum(e * dp.astype(f32), axis=0, keepdims=True)
                for n, j in enumerate(spans):
                    here = slice(n * sub, (n + 1) * sub)
                    totals[j] = totals[j] + part[:, here]
                    weights[j] = weights[j] + share[:, here]
        inv = 1.0 / jnp.concatenate(totals, axis=1)
        weighted = jnp.concatenate(weights, axis=1) * inv
        for b in range(3):
            for i in range(2):
                at = slice(b * toks + i * sub, b * toks + (i + 1) * sub)
                own = slice(i * sub, (i + 1) * sub)
                cols, spans = reach(b, i)
                p = e_s[at, cols] * inv[:, cols]
                ds = p * (dp_s[at, cols].astype(f32) - weighted[:, cols]) * query_scale
                ds = ds.astype(bf16)
                dv = jnp.dot(p.astype(bf16), go[cols], preferred_element_type=f32)
                dk = jnp.dot(ds, q[cols], preferred_element_type=f32)
                more = jnp.dot(blocks[b][0:HD, own], ds, preferred_element_type=f32)
                for n, j in enumerate(spans):
                    dqs[j] = dqs[j] + more[:, n * sub : (n + 1) * sub]
                if h == 0:
                    dk_s[at, :] = dk
                    dv_s[at, :] = dv
                else:
                    out = (d_m2_ref, d_m1_ref, d_own_ref)[b]
                    out[0, own, :] = (dk_s[at, :] + dk).astype(out.dtype)
                    out[1, own, :] = (dv_s[at, :] + dv).astype(out.dtype)
        dq_t = jnp.concatenate(dqs, axis=1)
        dq_low = dq_t.astype(bf16).astype(f32)
        dq_ref[rows, :] = unrotate_norm(dq_low, raw_ref[rows, :], qg_ref[...], cos, sin).astype(bf16)


def finish_kernel(dq_ref, own_ref, r1_ref, r2_ref, raw_ref, kg_ref, cos_ref, sin_ref, out_ref):
    def total(i):
        t = own_ref[i] + r1_ref[i].astype(f32) + r2_ref[i].astype(f32)
        return t.T.astype(bf16).astype(f32)

    out_ref[0 : 2 * HD, :] = dq_ref[...]
    out_ref[2 * HD : 3 * HD, :] = unrotate_norm(
        total(0), raw_ref[2 * HD : 3 * HD, :], kg_ref[...], cos_ref[...], sin_ref[...]
    ).astype(bf16)
    out_ref[3 * HD : 4 * HD, :] = total(1).astype(bf16)


def shards(hidden_in, w_query, w_key, w_value, q_gain, k_gain, grad_out):
    toks, feats = hidden_in.shape
    sds = jax.ShapeDtypeStruct
    ctx = lax.axis_index("ctx")
    tp = lax.axis_index("tp")
    core, j = ctx % NC, ctx // NC
    xh, y = tp // NY, tp % NY
    n_tp = NXH * NY
    blk = feats // 4

    def owner(rel):
        return ((xh + rel[0]) % NXH) * NY + (y + rel[1]) % NY

    positions = ctx * toks + lax.iota(jnp.int32, toks)
    freqs = jnp.exp(-math.log(rope_base) * (2.0 * jnp.arange(HALF, dtype=f32) / HD))
    angles = freqs[:, None] * positions.astype(f32)[None, :]
    cos, sin = jnp.cos(angles), jnp.sin(angles)
    qg, kg = q_gain[:, None], k_gain[:, None]

    w_cat = jnp.concatenate([w_query, w_key, w_value], axis=1)
    w_own = w_cat.reshape(n_tp, feats, w_cat.shape[1])

    table = jnp.stack([core, *[owner(rel) for rel in RELS + SENT], j // NZ]).astype(jnp.int32)
    w_last = lax.dynamic_index_in_dim(w_own, owner(RELS[7]), 0, keepdims=False).T

    def project(total, parts, rels):
        for xs, rel in zip(parts, rels):
            ws = lax.dynamic_index_in_dim(w_own, owner(rel), 0, keepdims=False)
            term = lax.dot_general(ws, xs, (((0,), (0,)), ((), ())), preferred_element_type=f32)
            total = term if total is None else total + term
        return total

    begun = []

    def for_both(parts):
        x = jnp.stack(parts).reshape(len(parts), 2, NC, blk, toks)
        return x, lax.dynamic_index_in_dim(x, 1 - core, 2, keepdims=False)

    def beside(parts):
        begun.append(project(None, parts, RELS[:4]))
        begun.append(for_both(parts))
        return begun[0], *begun[1], cos, sin, w_last, table

    x_parts = gather_tp(hidden_in.T, beside)
    most = project(begun[0], x_parts[4:7], RELS[4:7])
    xb, ob = for_both(x_parts[4:7])
    last, most, xb, ob = lax.optimization_barrier((x_parts[7], most, xb, ob))

    low = sds((2 * HD, toks), bf16)
    q_t, kv_t, raw = call(heads_kernel, (low, low, sds(most.shape, f32)), 2.5)(
        most, w_last, last, qg, kg, cos, sin
    )
    rings = [[(a * NZ + z) * NC + c for z in range(NZ)] for a in range(NXL) for c in range(NC)]

    def x_specs(at):
        return [
            pl.BlockSpec((1, 2, 1, blk, toks), lambda i, t: (at(i), 0, t[0], 0, 0)),
            pl.BlockSpec((1, 2, blk, toks), lambda i, t: (at(i), 0, 0, 0)),
        ]

    def pair_spec(first):
        half = 1 + len(RELS + SENT)
        return pl.BlockSpec(
            (1, 2, 1, blk, 2 * toks),
            lambda i, t: (t[first + i] % NY, 0, (t[first + i] // NY + t[half]) % NXL, 0, 0),
        )

    pair_shape = sds((NY, 2, NXH, blk, 2 * toks), bf16)

    def along_z(g):
        return lax.psum_scatter(
            g, "ctx", scatter_dimension=0, tiled=True, axis_index_groups=rings
        )[0]

    def across_x(g):
        g = g.reshape(NXL, blk, -1)
        outs = [sds((blk, w), f32) for w in (2 * HD, HD, HD)]
        return call(add_pair, outs, 0.7)(g, xlo_swap(g[1]))

    kv1 = from_behind(kv_t, 1)
    kv2 = from_behind(kv_t, 2)
    xa, oa = begun[1]
    joined = with_table(
        join_first,
        4.0,
        (4,),
        tie((table,), kv_t)[0],
        x_specs(lambda i: i),
        (xa, core_swap(oa)),
        pair_shape,
        pair_spec(1),
    )
    kv2, joined = lax.optimization_barrier((kv2, joined))
    xc, oc = for_both(tie((last,), kv_t))
    pair = sds((2, toks, HD), bf16)
    dq_raw, d_own, d1, d2 = call(
        attend_kernel,
        (sds((2 * HD, toks), bf16), sds((2, toks, HD), f32), pair, pair),
        5.5,
        (
            pltpu.VMEM((3 * toks, toks), f32),
            pltpu.VMEM((3 * toks, toks), bf16),
            pltpu.VMEM((3 * toks, HD), f32),
            pltpu.VMEM((3 * toks, HD), f32),
        ),
        smem_first=True,
    )(ctx[None], q_t, raw, kv_t, kv1, kv2, grad_out, qg, cos, sin)
    r1 = from_behind(d1, -1)
    r2 = from_behind(d2, -2)
    x_pair = with_table(
        join_rest,
        4.0,
        (4,),
        tie((table,), dq_raw)[0],
        [
            *x_specs(lambda i: jnp.minimum(i, 2)),
            *x_specs(lambda i: 0),
            pl.BlockSpec(memory_space=pl.ANY),
        ],
        (xb, core_swap(ob), xc, core_swap(oc), joined),
        pair_shape,
        pair_spec(5),
        alias={5: 0},
    ).reshape(NZ, NXL * blk, 2 * toks)
    r1, r2, x_pair = lax.optimization_barrier((r1, r2, x_pair))
    d_all = call(finish_kernel, sds((4 * HD, toks), bf16), 1.3)(
        dq_raw, d_own, r1, r2, raw, kg, cos, sin
    )
    d_other = core_swap(d_all)

    def beside_tail(after):
        here, there, _ = lax.optimization_barrier((d_all, d_other, after))
        d_pair = jnp.concatenate([here, there], axis=1)
        g = lax.dot_general(x_pair, d_pair, (((2,), (1,)), ((), ())), preferred_element_type=f32)
        return g.astype(bf16)

    grad_input, g = scatter_tp(w_own, d_all, table, beside_tail)
    grad_input = grad_input.T
    grad_w = across_x(along_z(g))
    return (grad_input, *grad_w)


def solution(mesh):
    placed = (P("ctx", "tp"), P(None, "tp"), P(None, "tp"), P(None, "tp"), P(), P(), P("ctx", "tp"))
    return jax.shard_map(
        shards,
        mesh=mesh,
        in_specs=placed,
        out_specs=(P("ctx", "tp"), P("ctx", "tp"), P("ctx", "tp"), P("ctx", "tp")),
        check_vma=False,
    )
```
